256 devices in a mesh: row: 16 (over z, y_lo), col: 16 (over y_hi, x, core).
Axes of the slice: x: 4, y: 4 (y_hi: 2, y_lo: 2; y = y_hi * 2 + y_lo), z: 8, core: 2. Of those that a mesh axis runs over, the one named last changes fastest.
Arguments:
- pair_map: bfloat16 [768, 768, 128], P('row', 'col'), may hold values from -6 to 6
- saved_product: bfloat16 [768, 768, 128], P('row', 'col'), may hold values from -6 to 6
- cotangent: bfloat16 [768, 768, 128], P('row', 'col'), may hold values from -1.5 to 1.5
- residue_mask: int32 [768], replicated, may hold values from 0 to 1, as said below
- ln_gain: float32 [128], replicated, may hold values from 0.25 to 1.75
- ln_bias: float32 [128], replicated, may hold values from -0.5 to 0.5
- out_gain: float32 [128], replicated, may hold values from 0.25 to 1.75
- out_bias: float32 [128], replicated, may hold values from -0.5 to 0.5
- w_a: bfloat16 [128, 128], replicated, may hold values from -0.5 to 0.5
- w_ag: bfloat16 [128, 128], replicated, may hold values from -0.5 to 0.5
- w_b: bfloat16 [128, 128], replicated, may hold values from -0.5 to 0.5
- w_bg: bfloat16 [128, 128], replicated, may hold values from -0.5 to 0.5
- w_g: bfloat16 [128, 128], replicated, may hold values from -0.5 to 0.5
- w_o: bfloat16 [128, 128], replicated, may hold values from -0.5 to 0.5
Outputs:
- grad_pair: bfloat16 [768, 768, 128], P('row', 'col')
- grad_w_a: float32 [128, 128], replicated
- grad_w_ag: float32 [128, 128], replicated
- grad_w_b: float32 [128, 128], replicated
- grad_w_bg: float32 [128, 128], replicated
- grad_w_g: float32 [128, 128], replicated
- grad_w_o: float32 [128, 128], replicated
- grad_ln_gain: float32 [128], replicated
- grad_ln_bias: float32 [128], replicated
- grad_out_gain: float32 [128], replicated
- grad_out_bias: float32 [128], replicated
The draws below stay inside these ranges and needn't reach their ends.
Inputs may be any that keep to these rules, and one draw needn't show every extreme that they name: `residue_mask`: between 1 and 192 residues are 0, anywhere in the crop.
All inputs are finite; a program needn't handle non-finite values.
Results may differ from the reference program's by a relative error of at most 0.02.
Values may be sent and summed in bfloat16 or wider, within the bound.
A program may use at most 128 MiB of HBM per device.

```python
import jax
import jax.numpy as jnp
from jax import lax

C = 128
N = 768
N_ROW = 16


def draw_residue_mask(key, part):
    key = jax.random.fold_in(key, 7)
    count_key, order_key = jax.random.split(key)
    padded = jax.random.randint(count_key, (), 1, N // 4 + 1)
    order = jax.random.permutation(order_key, N)
    return (order >= padded).astype(jnp.int32)


def block_scale(stream_key, extent, cuts, low, top_value):
    def one(axis_at, blocks):
        heights = jax.random.uniform(jax.random.fold_in(jax.random.fold_in(stream_key, 6), axis_at), (blocks,), jnp.float32, low / len(cuts), top_value / len(cuts))
        return jnp.repeat(jnp.exp(heights), extent[axis_at] // blocks).reshape((-1,) + (1,) * (len(extent) - axis_at - 1))

    level = one(*cuts[0])
    for cut in cuts[1:]:
        level = level * one(*cut)
    return level


def gaussian(stream_key, extent, spread, most, cuts=(), kind=jnp.bfloat16):
    values = spread * jax.random.normal(stream_key, extent, jnp.float32)
    if cuts:
        values = values * block_scale(stream_key, extent, cuts, -0.22, 0.18)
    return jnp.clip(values, -most, most).astype(kind)


def setup_inputs(seed: int = 0) -> dict:
    key_list = jax.random.split(jax.random.key(seed), 15)
    pair_map = gaussian(key_list[0], (N, N, C), 1.0, 6.0, ((0, 16), (1, 16)))
    saved_product = gaussian(key_list[1], (N, N, C), 1.0, 6.0, ((0, 16), (1, 16)))
    cotangent = gaussian(key_list[2], (N, N, C), 0.25, 1.5, ((0, 16), (1, 16)))
    residue_mask = draw_residue_mask(jax.random.fold_in(key_list[14], 71), 0)
    ln_gain = jnp.clip(1.0 + 0.15 * jax.random.normal(key_list[4], (C,), jnp.float32), 0.25, 1.75)
    ln_bias = jnp.clip(jax.random.uniform(key_list[5], (C,), jnp.float32, -0.5, 0.5), -0.5, 0.5)
    out_gain = jnp.clip(1.0 + 0.15 * jax.random.normal(key_list[6], (C,), jnp.float32), 0.25, 1.75)
    out_bias = jnp.clip(jax.random.uniform(key_list[7], (C,), jnp.float32, -0.5, 0.5), -0.5, 0.5)
    w_a = gaussian(key_list[8], (C, C), C ** -0.5, 0.5)
    w_ag = gaussian(key_list[9], (C, C), C ** -0.5, 0.5)
    w_b = gaussian(key_list[10], (C, C), C ** -0.5, 0.5)
    w_bg = gaussian(key_list[11], (C, C), C ** -0.5, 0.5)
    w_g = gaussian(key_list[12], (C, C), C ** -0.5, 0.5)
    w_o = gaussian(key_list[13], (C, C), C ** -0.5, 0.5)
    return dict(pair_map=pair_map, saved_product=saved_product, cotangent=cotangent, residue_mask=residue_mask, ln_gain=ln_gain, ln_bias=ln_bias, out_gain=out_gain, out_bias=out_bias, w_a=w_a, w_ag=w_ag, w_b=w_b, w_bg=w_bg, w_g=w_g, w_o=w_o)


epsilon = 1e-05

def normalize(values, gain_vec, bias_vec):
    values = values.astype(jnp.float32)
    centred = values - lax.optimization_barrier(jnp.mean(values, axis=-1, keepdims=True))
    inverse = lax.rsqrt(lax.optimization_barrier(jnp.mean(centred * centred, axis=-1, keepdims=True)) + epsilon)
    normed = centred * inverse
    return (normed * gain_vec + bias_vec, normed, inverse)

def norm_back(upstream, normed, inverse, gain_vec):
    scaled = upstream * gain_vec
    return inverse * (scaled - lax.optimization_barrier(jnp.mean(scaled, axis=-1, keepdims=True)) - normed * lax.optimization_barrier(jnp.mean(scaled * normed, axis=-1, keepdims=True)))

def project(values, matrix):
    flat = values.reshape(-1, values.shape[-1])
    result = jnp.dot(flat, matrix, preferred_element_type=jnp.float32)
    return result.reshape(values.shape[:-1] + (matrix.shape[1],))

def weight_grad(left, right):
    return jnp.dot(left.reshape(-1, left.shape[-1]).T, right.reshape(-1, right.shape[-1]), preferred_element_type=jnp.float32)

def channel_sum(values):
    return lax.optimization_barrier(jnp.sum(values, axis=(0, 1)))

def front(pair_map, saved_product, cotangent, pair_mask, ln_gain, ln_bias, out_gain, out_bias, w_a, w_ag, w_b, w_bg, w_g, w_o):
    pair_full, pair_hat, pair_inv = normalize(pair_map, ln_gain, ln_bias)
    normed_pair = pair_full.astype(jnp.bfloat16)
    proj_a = project(normed_pair, w_a)
    sig_a = jax.nn.sigmoid(project(normed_pair, w_ag))
    proj_b = project(normed_pair, w_b)
    sig_b = jax.nn.sigmoid(project(normed_pair, w_bg))
    gate_value = jax.nn.sigmoid(project(normed_pair, w_g))
    factor_a = (pair_mask * sig_a * proj_a).astype(jnp.bfloat16)
    factor_b = (pair_mask * sig_b * proj_b).astype(jnp.bfloat16)
    out_full, out_hat, out_inv = normalize(saved_product, out_gain, out_bias)
    normed_out = out_full.astype(jnp.bfloat16)
    update = project(normed_out, w_o)
    upstream = cotangent.astype(jnp.float32)
    grad_update = (upstream * gate_value).astype(jnp.bfloat16)
    grad_gate = (upstream * update * gate_value * (1.0 - gate_value)).astype(jnp.bfloat16)
    grad_normed_out = project(grad_update, w_o.T)
    grad_saved = norm_back(grad_normed_out, out_hat, out_inv, out_gain).astype(jnp.bfloat16)
    early = (weight_grad(normed_pair, grad_gate), weight_grad(normed_out, grad_update), channel_sum(grad_normed_out * out_hat), channel_sum(grad_normed_out))
    kept = (normed_pair, pair_hat, pair_inv, proj_a, sig_a, proj_b, sig_b, grad_gate)
    return (factor_a, factor_b, grad_saved, early, kept)

def back(grad_fa, grad_fb, pair_mask, kept, ln_gain, w_a, w_ag, w_b, w_bg, w_g):
    normed_pair, pair_hat, pair_inv, proj_a, sig_a, proj_b, sig_b, grad_gate = kept
    masked_a = grad_fa * pair_mask
    masked_b = grad_fb * pair_mask
    grad_pa = (masked_a * sig_a).astype(jnp.bfloat16)
    grad_pag = (masked_a * proj_a * sig_a * (1.0 - sig_a)).astype(jnp.bfloat16)
    grad_pb = (masked_b * sig_b).astype(jnp.bfloat16)
    grad_pbg = (masked_b * proj_b * sig_b * (1.0 - sig_b)).astype(jnp.bfloat16)
    grad_zn = project(grad_pa, w_a.T) + project(grad_pag, w_ag.T) + project(grad_pb, w_b.T) + project(grad_pbg, w_bg.T) + project(grad_gate, w_g.T)
    grad_pair = norm_back(grad_zn, pair_hat, pair_inv, ln_gain).astype(jnp.bfloat16)
    late = (weight_grad(normed_pair, grad_pa), weight_grad(normed_pair, grad_pag), weight_grad(normed_pair, grad_pb), weight_grad(normed_pair, grad_pbg), channel_sum(grad_zn * pair_hat), channel_sum(grad_zn))
    return (grad_pair, late)

def reference(pair_map, saved_product, cotangent, residue_mask, ln_gain, ln_bias, out_gain, out_bias, w_a, w_ag, w_b, w_bg, w_g, w_o):
    residue_float = residue_mask.astype(jnp.float32)
    pair_mask = (residue_float[:, None] * residue_float[None, :])[:, :, None]
    factor_a, factor_b, grad_saved, early, kept = front(pair_map, saved_product, cotangent, pair_mask, ln_gain, ln_bias, out_gain, out_bias, w_a, w_ag, w_b, w_bg, w_g, w_o)
    upstream_t = grad_saved.astype(jnp.float32).transpose(2, 0, 1)
    right_t = factor_b.astype(jnp.float32).transpose(2, 0, 1)
    left_t = factor_a.astype(jnp.float32).transpose(2, 0, 1)
    grad_fa = jnp.matmul(upstream_t, right_t).transpose(1, 2, 0)
    block_rows = N // N_ROW
    upstream_blocks = upstream_t.reshape(C, N_ROW, block_rows, N).transpose(1, 0, 2, 3)
    left_blocks = left_t.reshape(C, N_ROW, block_rows, N).transpose(1, 0, 2, 3)

    def add_block(running, blocks):
        upstream_block, left_block = blocks
        block_sum = jnp.matmul(upstream_block.transpose(0, 2, 1), left_block)
        block_sum = lax.optimization_barrier(block_sum.astype(jnp.bfloat16)).astype(jnp.float32)
        return (running + block_sum, None)
    summed, _ = lax.scan(add_block, jnp.zeros((C, N, N), jnp.float32), (upstream_blocks, left_blocks))
    grad_fb = summed.transpose(1, 2, 0)
    grad_pair, late = back(grad_fa, grad_fb, pair_mask, kept, ln_gain, w_a, w_ag, w_b, w_bg, w_g)
    inv_total = 1.0 / N
    return (grad_pair, late[0] * inv_total, late[1] * inv_total, late[2] * inv_total, late[3] * inv_total, early[0] * inv_total, early[1] * inv_total, late[4] * inv_total, late[5] * inv_total, early[2] * inv_total, early[3] * inv_total)
```

```python
import jax
import jax.numpy as jnp
from jax import lax
from jax.experimental import pallas as pl
from jax.experimental.pallas import tpu as pltpu
from jax.sharding import PartitionSpec as P

MESH = pl.DeviceIdType.MESH
f32 = jnp.float32
bf16 = jnp.bfloat16
epsilon = 1e-05
VMEM = pl.BlockSpec(memory_space=pltpu.VMEM)
LIMIT = 56 << 20

DEV = 16
BLK = 48
CH = 128
PACK = 8
GROUPS = BLK // PACK
LANES = PACK * BLK
TILES = LANES // 128
CPD = CH // DEV
ROWS = GROUPS * CPD
CROWS = GROUPS * DEV
N = DEV * BLK
STEP = 16
CELLS = STEP * BLK
NSTEP = BLK // STEP
SUMROWS = 64


def dot(a, b, ca=1, cb=0):
    return lax.dot_general(a, b, (((ca,), (cb,)), ((), ())), preferred_element_type=f32)


def mean(v):
    return jnp.mean(v, axis=-1, keepdims=True)


def normalize(values):
    values = values.astype(f32)
    centred = values - mean(values)
    inverse = lax.rsqrt(mean(centred * centred) + epsilon)
    return centred * inverse, inverse


def norm_back(scaled, normed, inverse):
    return inverse * (scaled - mean(scaled) - normed * mean(scaled * normed))


def to_channels(ref, values):
    halves = []
    for g in range(STEP // PACK):
        turned = values[g * LANES : (g + 1) * LANES].T
        halves.append(turned.reshape(DEV, CPD, LANES))
    ref[...] = jnp.concatenate(halves, axis=1).astype(bf16)


def from_channels(ref):
    values = ref[...].astype(f32)
    parts = []
    for g in range(STEP // PACK):
        parts.append(values[:, g * CPD : (g + 1) * CPD, :].reshape(CH, LANES).T)
    return jnp.concatenate(parts, axis=0)


def front_kernel(
    pm, sp, ct, rm, km, vec, wcat, wo, gx_t, fa_t, fb_t, a1, a2, b1, b2, gg, gwo, gvec
):
    step = pl.program_id(0)
    mask = jnp.broadcast_to(rm[...][:, None, :] * km[...][None], (STEP, BLK, CH)).reshape(CELLS, CH)
    ln_gain, ln_bias, out_gain, out_bias = (vec[i : i + 1, :] for i in range(4))
    hat, _ = normalize(pm[...].reshape(CELLS, CH))
    zn = (hat * ln_gain + ln_bias).astype(bf16)
    pa, pag, pb, pbg, pg = (dot(zn, wcat[:, i * CH : (i + 1) * CH]) for i in range(5))
    sig_a = jax.nn.sigmoid(pag)
    ma = mask * sig_a
    fa = ma * pa
    a1[...] = ma
    a2[...] = fa * (1.0 - sig_a)
    to_channels(fa_t, fa)
    sig_b = jax.nn.sigmoid(pbg)
    mb = mask * sig_b
    fb = mb * pb
    b1[...] = mb
    b2[...] = fb * (1.0 - sig_b)
    to_channels(fb_t, fb)
    gate = jax.nn.sigmoid(pg)
    ohat, oinv = normalize(sp[...].reshape(CELLS, CH))
    xn = (ohat * out_gain + out_bias).astype(bf16)
    update = dot(xn, wo[...])
    up = ct[...].reshape(CELLS, CH).astype(f32) * gate
    gu = up.astype(bf16)
    gg[...] = (up * update * (1.0 - gate)).astype(bf16)
    gxn = dot(gu, wo[...], 1, 1)
    to_channels(gx_t, norm_back(gxn * out_gain, ohat, oinv))
    gw = dot(xn, gu, 0, 0)
    sums = jnp.concatenate(
        [
            jnp.sum(gxn * ohat, axis=0, keepdims=True),
            jnp.sum(gxn, axis=0, keepdims=True),
            jnp.zeros((6, CH), f32),
        ],
        axis=0,
    )

    @pl.when(step == 0)
    def _():
        gwo[...] = gw
        gvec[...] = sums

    @pl.when(step > 0)
    def _():
        gwo[...] += gw
        gvec[...] += sums


def whole(*shape):
    return pl.BlockSpec(shape, lambda i: (0,) * len(shape))


def front(pm, sp, ct, rm, km, vec, wcat, wo):
    cells = pl.BlockSpec((STEP, BLK, CH), lambda i: (i, 0, 0))
    flat = pl.BlockSpec((CELLS, CH), lambda i: (i, 0))
    turned = pl.BlockSpec((DEV, STEP // PACK * CPD, LANES), lambda i: (0, i, 0))
    t_shape = jax.ShapeDtypeStruct((DEV, ROWS, LANES), bf16)
    c_shape = jax.ShapeDtypeStruct((BLK * BLK, CH), f32)
    return pl.pallas_call(
        front_kernel,
        grid=(NSTEP,),
        in_specs=[
            cells,
            cells,
            cells,
            pl.BlockSpec((STEP, CH), lambda i: (i, 0)),
            whole(BLK, CH),
            whole(8, CH),
            whole(CH, 5 * CH),
            whole(CH, CH),
        ],
        out_specs=[turned] * 3 + [flat] * 5 + [whole(CH, CH), whole(8, CH)],
        out_shape=[t_shape] * 3
        + [c_shape] * 4
        + [
            jax.ShapeDtypeStruct((BLK * BLK, CH), bf16),
            jax.ShapeDtypeStruct((CH, CH), f32),
            jax.ShapeDtypeStruct((8, CH), f32),
        ],
        name="front",
        compiler_params=pltpu.CompilerParams(vmem_limit_bytes=LIMIT),
    )(pm, sp, ct, rm, km, vec, wcat, wo)


def back_kernel(pm, gfa, gfb, a1, a2, b1, b2, gg, vec, wcat, gp, gw, gvec):
    step = pl.program_id(0)
    ln_gain, ln_bias = vec[0:1, :], vec[1:2, :]
    hat, inv = normalize(pm[...].reshape(CELLS, CH))
    zn = (hat * ln_gain + ln_bias).astype(bf16)
    ga = from_channels(gfa)
    gb = from_channels(gfb)
    grads = jnp.concatenate(
        [
            (ga * a1[...]).astype(bf16),
            (ga * a2[...]).astype(bf16),
            (gb * b1[...]).astype(bf16),
            (gb * b2[...]).astype(bf16),
            gg[...],
        ],
        axis=1,
    )
    gz = dot(grads, wcat[...], 1, 1)
    gp[...] = norm_back(gz * ln_gain, hat, inv).astype(bf16).reshape(STEP, BLK, CH)
    part = dot(zn, grads, 0, 0)
    sums = jnp.concatenate(
        [
            jnp.sum(gz * hat, axis=0, keepdims=True),
            jnp.sum(gz, axis=0, keepdims=True),
            jnp.zeros((6, CH), f32),
        ],
        axis=0,
    )

    @pl.when(step == 0)
    def _():
        gw[...] = part
        gvec[...] = sums

    @pl.when(step > 0)
    def _():
        gw[...] += part
        gvec[...] += sums


def back(pm, gfa, gfb, a1, a2, b1, b2, gg, vec, wcat):
    cells = pl.BlockSpec((STEP, BLK, CH), lambda i: (i, 0, 0))
    flat = pl.BlockSpec((CELLS, CH), lambda i: (i, 0))
    turned = pl.BlockSpec((DEV, STEP // PACK * CPD, LANES), lambda i: (0, i, 0))
    return pl.pallas_call(
        back_kernel,
        grid=(NSTEP,),
        in_specs=[cells, turned, turned] + [flat] * 5 + [whole(8, CH), whole(CH, 5 * CH)],
        out_specs=[cells, whole(CH, 5 * CH), whole(8, CH)],
        out_shape=[
            jax.ShapeDtypeStruct((BLK, BLK, CH), bf16),
            jax.ShapeDtypeStruct((CH, 5 * CH), f32),
            jax.ShapeDtypeStruct((8, CH), f32),
        ],
        name="back",
        compiler_params=pltpu.CompilerParams(vmem_limit_bytes=LIMIT),
    )(pm, gfa, gfb, a1, a2, b1, b2, gg, vec, wcat)


def peer(axis, d):
    return lax.rem(lax.axis_index(axis) + d, DEV)


def greet(axes):
    barrier = pltpu.get_barrier_semaphore()
    for axis in axes:

        def hello(d, carry):
            pl.semaphore_signal(
                barrier, inc=1, device_id={axis: peer(axis, d)}, device_id_type=MESH
            )
            return carry

        lax.fori_loop(1, DEV, hello, 0)
    pl.semaphore_wait(barrier, len(axes) * (DEV - 1))


def each(action):
    def run(d, carry):
        action(d)
        return carry

    lax.fori_loop(1, DEV, run, 0)


def copier(axis, src, dst, send, recv):
    def make(d):
        t = peer(axis, d)
        return pltpu.make_async_remote_copy(
            src_ref=src(t),
            dst_ref=dst,
            send_sem=send.at[d],
            recv_sem=recv.at[d],
            device_id={axis: t},
            device_id_type=MESH,
        )

    return make


def there_kernel(
    gx, fa, fb, gout, fout, rbuf, scr, sbuf, r_send, r_recv, c_send, c_recv, r_loc, c_loc
):
    row, col = lax.axis_index("row"), lax.axis_index("col")
    arrays = (gx, fa, fb)
    own = [
        pltpu.make_async_copy(arrays[a].at[row], rbuf.at[a, row], r_loc.at[a]) for a in range(3)
    ]
    for o in own:
        o.start()
    greet(("row", "col"))
    rows = [
        copier(
            "row",
            lambda t, a=a: arrays[a].at[t],
            rbuf.at[a, row],
            r_send.at[a],
            r_recv.at[a],
        )
        for a in range(3)
    ]
    for a in range(3):
        each(lambda d, a=a: rows[a](d).start())

    def shuffle(a):
        own[a].wait()
        each(lambda d: rows[a](d).wait_recv())
        for t in range(TILES):
            lanes = slice(t * 128, (t + 1) * 128)
            scr[t] = rbuf[a, :, :, lanes].reshape(DEV * ROWS, 128).astype(f32)
            for m in range(CPD):
                sbuf[a, m, :, lanes] = scr[t, pl.ds(m, CROWS, stride=CPD), :].astype(bf16)

    g_copy = copier("col", lambda t: sbuf.at[0, t // 2], gout.at[col], c_send.at[0], c_recv.at[0])
    f_copy = copier(
        "col",
        lambda t: sbuf.at[2 - lax.rem(t, 2), t // 2],
        fout.at[col],
        c_send.at[1],
        c_recv.at[1],
    )
    shuffle(0)
    own_g = pltpu.make_async_copy(sbuf.at[0, col // 2], gout.at[col], c_loc.at[0])
    own_g.start()
    each(lambda d: g_copy(d).start())
    shuffle(1)
    shuffle(2)
    own_f = pltpu.make_async_copy(sbuf.at[2 - lax.rem(col, 2), col // 2], fout.at[col], c_loc.at[1])
    own_f.start()
    each(lambda d: f_copy(d).start())
    for a in range(3):
        each(lambda d, a=a: rows[a](d).wait_send())
    own_g.wait()
    each(lambda d: g_copy(d).wait())
    own_f.wait()
    each(lambda d: f_copy(d).wait())


def there(gx, fa, fb):
    shape = jax.ShapeDtypeStruct((DEV, CROWS, LANES), bf16)
    dma = pltpu.SemaphoreType.DMA
    return pl.pallas_call(
        there_kernel,
        in_specs=[VMEM] * 3,
        out_specs=[VMEM] * 2,
        out_shape=[shape] * 2,
        scratch_shapes=[
            pltpu.VMEM((3, DEV, ROWS, LANES), bf16),
            pltpu.VMEM((TILES, DEV * ROWS, 128), f32),
            pltpu.VMEM((3, CPD, CROWS, LANES), bf16),
            dma((3, DEV)),
            dma((3, DEV)),
            dma((2, DEV)),
            dma((2, DEV)),
            dma((3,)),
            dma((2,)),
        ],
        name="there",
        compiler_params=pltpu.CompilerParams(
            collective_id=1, has_side_effects=True, vmem_limit_bytes=LIMIT
        ),
    )(gx, fa, fb)


def home_kernel(g, ga, gb, cbuf, scr, sbuf, c_send, c_recv, r_send, r_recv, loc):
    row, col = lax.axis_index("row"), lax.axis_index("col")
    outs = (ga, gb)
    own = pltpu.make_async_copy(g.at[col], cbuf.at[col], loc.at[0])
    own.start()
    greet(("row", "col"))
    cols = copier("col", lambda t: g.at[t], cbuf.at[col], c_send, c_recv)
    each(lambda d: cols(d).start())
    own.wait()
    each(lambda d: cols(d).wait_recv())
    rows = [
        copier(
            "row", lambda t, h=h: sbuf.at[h, t], outs[h].at[row], r_send.at[h], r_recv.at[h]
        )
        for h in range(2)
    ]
    mine = []
    for h in range(2):
        for t in range(TILES):
            lanes = slice(t * 128, (t + 1) * 128)
            for m in range(CPD):
                scr[t, pl.ds(m, CROWS, stride=CPD), :] = cbuf[2 * m + h, :, lanes].astype(f32)
            sbuf[h, :, :, lanes] = scr[t].reshape(DEV, ROWS, 128).astype(bf16)
        mine.append(pltpu.make_async_copy(sbuf.at[h, row], outs[h].at[row], loc.at[1 + h]))
        mine[h].start()
        each(lambda d, h=h: rows[h](d).start())
    each(lambda d: cols(d).wait_send())
    for h in range(2):
        mine[h].wait()
        each(lambda d, h=h: rows[h](d).wait())


def home(g):
    shape = jax.ShapeDtypeStruct((DEV, ROWS, LANES), bf16)
    dma = pltpu.SemaphoreType.DMA
    return pl.pallas_call(
        home_kernel,
        in_specs=[VMEM],
        out_specs=[VMEM] * 2,
        out_shape=[shape] * 2,
        scratch_shapes=[
            pltpu.VMEM((DEV, CROWS, LANES), bf16),
            pltpu.VMEM((TILES, DEV * ROWS, 128), f32),
            pltpu.VMEM((2, DEV, ROWS, LANES), bf16),
            dma((DEV,)),
            dma((DEV,)),
            dma((2, DEV)),
            dma((2, DEV)),
            dma((3,)),
        ],
        name="home",
        compiler_params=pltpu.CompilerParams(
            collective_id=2, has_side_effects=True, vmem_limit_bytes=LIMIT
        ),
    )(g)


NT = N // 128


def assemble(src, scr, dst):
    for a in range(PACK):
        rows = jnp.concatenate(
            [src[q][:, a * BLK : (a + 1) * BLK].astype(f32) for q in range(DEV)], axis=1
        )
        for t in range(NT):
            scr[t, pl.ds(a, CROWS, stride=PACK), :] = rows[:, t * 128 : (t + 1) * 128]
    for t in range(NT):
        dst[:, t * 128 : (t + 1) * 128] = scr[t].astype(bf16)


def product_kernel(g, f, out, scr, gfull, ffull):
    assemble(g, scr, gfull)
    assemble(f, scr, ffull)
    odd = lax.rem(lax.axis_index("col"), 2)

    def spread(values):
        for t in range(NT):
            scr[t] = values[:, t * 128 : (t + 1) * 128]

    @pl.when(odd == 0)
    def _():
        spread(dot(gfull[...], ffull[...]))

    @pl.when(odd == 1)
    def _():
        spread(dot(gfull[...], ffull[...], 0, 0))

    rows = [[scr[t, pl.ds(a, CROWS, stride=PACK), :] for t in range(NT)] for a in range(PACK)]

    def piece(a, q):
        lo, hi = q * BLK, (q + 1) * BLK
        first, last = lo // 128, (hi - 1) // 128
        if first == last:
            return rows[a][first][:, lo - first * 128 : hi - first * 128]
        return jnp.concatenate(
            [rows[a][first][:, lo - first * 128 :], rows[a][last][:, : hi - last * 128]], axis=1
        )

    for q in range(DEV):
        out[q] = jnp.concatenate([piece(a, q) for a in range(PACK)], axis=1).astype(bf16)


def product(g, f):
    return pl.pallas_call(
        product_kernel,
        in_specs=[VMEM] * 2,
        out_specs=VMEM,
        out_shape=jax.ShapeDtypeStruct((DEV, CROWS, LANES), bf16),
        scratch_shapes=[
            pltpu.VMEM((NT, N, 128), f32),
            pltpu.VMEM((N, N), bf16),
            pltpu.VMEM((N, N), bf16),
        ],
        name="product",
        compiler_params=pltpu.CompilerParams(vmem_limit_bytes=LIMIT),
    )(g, f)


def sum_kernel(gw, gwo, gvec, lvec, out, part, got1, mid, got2, fin, sem_s, sem_r, loc):
    row, col = lax.axis_index("row"), lax.axis_index("col")
    for k in range(5):
        for j in range(2):
            part[2 * k + j] = gw[j * 64 : (j + 1) * 64, k * CH : (k + 1) * CH].astype(bf16)
    for j in range(2):
        part[10 + j] = gwo[j * 64 : (j + 1) * 64, :].astype(bf16)
    part[12] = jnp.concatenate(
        [lvec[...], gvec[...], jnp.zeros((SUMROWS - 16, CH), f32)], axis=0
    ).astype(bf16)
    part[13:16] = jnp.zeros((3, SUMROWS, CH), bf16)
    own = pltpu.make_async_copy(part.at[col], got1.at[col], loc.at[0])
    own.start()
    greet(("row", "col"))
    one = copier("col", lambda t: part.at[t], got1.at[col], sem_s.at[0], sem_r.at[0])
    each(lambda d: one(d).start())
    own.wait()
    each(lambda d: one(d).wait())
    mid[...] = jnp.sum(got1[...].astype(f32), axis=0).astype(bf16)
    own = pltpu.make_async_copy(mid, got2.at[row], loc.at[1])
    own.start()
    two = copier("row", lambda t: mid, got2.at[row], sem_s.at[1], sem_r.at[1])
    each(lambda d: two(d).start())
    own.wait()
    each(lambda d: two(d).wait())
    fin[...] = (jnp.sum(got2[...].astype(f32), axis=0) * (1.0 / N)).astype(bf16)
    own = pltpu.make_async_copy(fin, out.at[col], loc.at[2])
    own.start()
    three = copier("col", lambda t: fin, out.at[col], sem_s.at[2], sem_r.at[2])
    each(lambda d: three(d).start())
    own.wait()
    each(lambda d: three(d).wait())


def sum_all(gw, gwo, gvec, lvec):
    dma = pltpu.SemaphoreType.DMA
    wide = (DEV, SUMROWS, CH)
    return pl.pallas_call(
        sum_kernel,
        in_specs=[VMEM] * 4,
        out_specs=VMEM,
        out_shape=jax.ShapeDtypeStruct(wide, bf16),
        scratch_shapes=[
            pltpu.VMEM(wide, bf16),
            pltpu.VMEM(wide, bf16),
            pltpu.VMEM((SUMROWS, CH), bf16),
            pltpu.VMEM(wide, bf16),
            pltpu.VMEM((SUMROWS, CH), bf16),
            dma((3, DEV)),
            dma((3, DEV)),
            dma((3,)),
        ],
        name="sum_all",
        compiler_params=pltpu.CompilerParams(
            collective_id=3, has_side_effects=True, vmem_limit_bytes=LIMIT
        ),
    )(gw, gwo, gvec, lvec)


def finish_kernel(s, *outs):
    for k in range(6):
        for j in range(2):
            outs[k][j * 64 : (j + 1) * 64, :] = s[2 * k + j].astype(f32)
    vec = s[12].astype(f32)
    outs[6][...] = vec[0:1]
    outs[7][...] = vec[1:2]
    outs[8][...] = vec[8:9]
    outs[9][...] = vec[9:10]


def finish(s):
    return pl.pallas_call(
        finish_kernel,
        in_specs=[VMEM],
        out_specs=[VMEM] * 10,
        out_shape=[jax.ShapeDtypeStruct((CH, CH), f32)] * 6
        + [jax.ShapeDtypeStruct((1, CH), f32)] * 4,
        name="finish",
    )(s)


def body(
    pair_map,
    saved_product,
    cotangent,
    residue_mask,
    ln_gain,
    ln_bias,
    out_gain,
    out_bias,
    w_a,
    w_ag,
    w_b,
    w_bg,
    w_g,
    w_o,
):
    row_first = lax.axis_index("row") * BLK
    col_first = lax.axis_index("col") * BLK
    row_mask = lax.dynamic_slice_in_dim(residue_mask, row_first, BLK, 0).astype(f32)
    col_mask = lax.dynamic_slice_in_dim(residue_mask, col_first, BLK, 0).astype(f32)
    rm = jnp.broadcast_to(row_mask[:, None], (BLK, CH))
    km = jnp.broadcast_to(col_mask[:, None], (BLK, CH))
    vec = jnp.concatenate(
        [jnp.stack([ln_gain, ln_bias, out_gain, out_bias]), jnp.zeros((4, CH), f32)], axis=0
    )
    wcat = jnp.concatenate([w_a, w_ag, w_b, w_bg, w_g], axis=1)
    gx, fa, fb, a1, a2, b1, b2, gg, gwo, gvec = front(
        pair_map, saved_product, cotangent, rm, km, vec, wcat, w_o
    )
    gall, fall = there(gx, fa, fb)
    gfa, gfb = home(product(gall, fall))
    grad_pair, gw, lvec = back(pair_map, gfa, gfb, a1, a2, b1, b2, gg, vec, wcat)
    outs = finish(sum_all(gw, gwo, gvec, lvec))
    return (grad_pair,) + tuple(outs[:6]) + tuple(v.reshape(CH) for v in outs[6:])


def solution(mesh):
    return jax.shard_map(
        body,
        mesh=mesh,
        in_specs=(P("row", "col", None),) * 3 + (P(),) * 11,
        out_specs=(P("row", "col", None),) + (P(),) * 10,
        check_vma=False,
    )
```

```python
import jax
import jax.numpy as jnp
from jax import lax
from jax.experimental import pallas as pl
from jax.experimental.pallas import tpu as pltpu
from jax.sharding import PartitionSpec as P

MESH = pl.DeviceIdType.MESH
f32 = jnp.float32
bf16 = jnp.bfloat16
epsilon = 1e-05
VMEM = pl.BlockSpec(memory_space=pltpu.VMEM)
LIMIT = 56 << 20

DEV = 16
BLK = 48
CH = 128
PACK = 8
GROUPS = BLK // PACK
LANES = PACK * BLK
TILES = LANES // 128
CPD = CH // DEV
ROWS = GROUPS * CPD
CROWS = GROUPS * DEV
N = DEV * BLK
STEP = 16
CELLS = STEP * BLK
NSTEP = BLK // STEP
SUMROWS = 64
PROWS = STEP // PACK * CPD
CPROWS = STEP // PACK * DEV
PN = STEP * DEV
NT = N // 128


def dot(a, b, ca=1, cb=0):
    return lax.dot_general(a, b, (((ca,), (cb,)), ((), ())), preferred_element_type=f32)


def mean(v):
    return jnp.mean(v, axis=-1, keepdims=True)


def normalize(values):
    values = values.astype(f32)
    centred = values - mean(values)
    inverse = lax.rsqrt(mean(centred * centred) + epsilon)
    return centred * inverse, inverse


def norm_back(scaled, normed, inverse):
    return inverse * (scaled - mean(scaled) - normed * mean(scaled * normed))


def to_channels(ref, values):
    halves = []
    for g in range(STEP // PACK):
        turned = values[g * LANES : (g + 1) * LANES].T
        halves.append(turned.reshape(DEV, CPD, LANES))
    ref[...] = jnp.concatenate(halves, axis=1).astype(bf16)[None]


def from_channels(ref):
    values = ref[0].astype(f32)
    parts = []
    for g in range(STEP // PACK):
        parts.append(values[:, g * CPD : (g + 1) * CPD, :].reshape(CH, LANES).T)
    return jnp.concatenate(parts, axis=0)


def mask_of(rmask, axis):
    first = lax.axis_index(axis) * BLK
    lane = lax.broadcasted_iota(jnp.int32, (BLK, N), 1)
    sub = lax.broadcasted_iota(jnp.int32, (BLK, N), 0)
    picked = jnp.where(lane == sub + first, rmask[...].astype(f32), 0.0)
    return jnp.broadcast_to(jnp.sum(picked, axis=1, keepdims=True), (BLK, CH))


def front_kernel(
    pm, sp, ct, rmask, lg, lb, og, ob, wa, wag, wb, wbg, wg, wo,
    gx_t, fa_t, fb_t, a1, a2, b1, b2, gg, gwo, gvec, rm, km,
):
    step = pl.program_id(0)

    @pl.when(step == 0)
    def _():
        rm[...] = mask_of(rmask, "row")
        km[...] = mask_of(rmask, "col")

    rows = rm[pl.ds(pl.multiple_of(step * STEP, STEP), STEP), :]
    mask = jnp.broadcast_to(rows[:, None, :] * km[...][None], (STEP, BLK, CH)).reshape(CELLS, CH)
    hat, _ = normalize(pm[...].reshape(CELLS, CH))
    zn = (hat * lg[...] + lb[...]).astype(bf16)
    ohat, oinv = normalize(sp[...].reshape(CELLS, CH))
    xn = (ohat * og[...] + ob[...]).astype(bf16)
    gate = jax.nn.sigmoid(dot(zn, wg[...]))
    update = dot(xn, wo[...])
    up = ct[...].reshape(CELLS, CH).astype(f32) * gate
    gu = up.astype(bf16)
    gg[...] = (up * update * (1.0 - gate)).astype(bf16)
    gxn = dot(gu, wo[...], 1, 1)
    to_channels(gx_t, norm_back(gxn * og[...], ohat, oinv))
    sig_a = jax.nn.sigmoid(dot(zn, wag[...]))
    ma = mask * sig_a
    fa = ma * dot(zn, wa[...])
    a1[...] = ma
    a2[...] = fa * (1.0 - sig_a)
    to_channels(fa_t, fa)
    sig_b = jax.nn.sigmoid(dot(zn, wbg[...]))
    mb = mask * sig_b
    fb = mb * dot(zn, wb[...])
    b1[...] = mb
    b2[...] = fb * (1.0 - sig_b)
    to_channels(fb_t, fb)
    gw = dot(xn, gu, 0, 0)
    sums = jnp.concatenate(
        [
            jnp.sum(gxn * ohat, axis=0, keepdims=True),
            jnp.sum(gxn, axis=0, keepdims=True),
            jnp.zeros((6, CH), f32),
        ],
        axis=0,
    )

    @pl.when(step == 0)
    def _():
        gwo[...] = gw
        gvec[...] = sums

    @pl.when(step > 0)
    def _():
        gwo[...] += gw
        gvec[...] += sums


def whole(*shape):
    return pl.BlockSpec(shape, lambda i: (0,) * len(shape))


def specs():
    cells = pl.BlockSpec((STEP, BLK, CH), lambda i: (i, 0, 0))
    flat = pl.BlockSpec((CELLS, CH), lambda i: (i, 0))
    turned = pl.BlockSpec((1, DEV, PROWS, LANES), lambda i: (i, 0, 0, 0))
    return cells, flat, turned


TURNED = jax.ShapeDtypeStruct((NSTEP, DEV, PROWS, LANES), bf16)


def front(pm, sp, ct, rmask, vecs, weights):
    cells, flat, turned = specs()
    c_shape = jax.ShapeDtypeStruct((BLK * BLK, CH), f32)
    return pl.pallas_call(
        front_kernel,
        grid=(NSTEP,),
        in_specs=[cells] * 3 + [whole(1, N)] + [whole(1, CH)] * 4 + [whole(CH, CH)] * 6,
        out_specs=[turned] * 3 + [flat] * 5 + [whole(CH, CH), whole(8, CH)],
        out_shape=[TURNED] * 3
        + [c_shape] * 4
        + [
            jax.ShapeDtypeStruct((BLK * BLK, CH), bf16),
            jax.ShapeDtypeStruct((CH, CH), f32),
            jax.ShapeDtypeStruct((8, CH), f32),
        ],
        scratch_shapes=[pltpu.VMEM((BLK, CH), f32)] * 2,
        name="front",
        compiler_params=pltpu.CompilerParams(vmem_limit_bytes=LIMIT),
    )(pm, sp, ct, rmask, *vecs, *weights)


def back_kernel(
    pm, gfa, gfb, a1, a2, b1, b2, gg, lg, lb, wa, wag, wb, wbg, wg, gp, gw, gvec, wcat
):
    step = pl.program_id(0)

    @pl.when(step == 0)
    def _():
        for k, w in enumerate((wa, wag, wb, wbg, wg)):
            wcat[:, k * CH : (k + 1) * CH] = w[...]

    hat, inv = normalize(pm[...].reshape(CELLS, CH))
    zn = (hat * lg[...] + lb[...]).astype(bf16)
    ga = from_channels(gfa)
    gb = from_channels(gfb)
    grads = jnp.concatenate(
        [
            (ga * a1[...]).astype(bf16),
            (ga * a2[...]).astype(bf16),
            (gb * b1[...]).astype(bf16),
            (gb * b2[...]).astype(bf16),
            gg[...],
        ],
        axis=1,
    )
    gz = dot(grads, wcat[...], 1, 1)
    gp[...] = norm_back(gz * lg[...], hat, inv).astype(bf16).reshape(STEP, BLK, CH)
    part = dot(zn, grads, 0, 0)
    sums = jnp.concatenate(
        [
            jnp.sum(gz * hat, axis=0, keepdims=True),
            jnp.sum(gz, axis=0, keepdims=True),
            jnp.zeros((6, CH), f32),
        ],
        axis=0,
    )

    @pl.when(step == 0)
    def _():
        gw[...] = part
        gvec[...] = sums

    @pl.when(step > 0)
    def _():
        gw[...] += part
        gvec[...] += sums


def back(pm, gfa, gfb, a1, a2, b1, b2, gg, vecs, weights):
    cells, flat, turned = specs()
    return pl.pallas_call(
        back_kernel,
        grid=(NSTEP,),
        in_specs=[cells, turned, turned]
        + [flat] * 5
        + [whole(1, CH)] * 2
        + [whole(CH, CH)] * 5,
        out_specs=[cells, whole(CH, 5 * CH), whole(8, CH)],
        out_shape=[
            jax.ShapeDtypeStruct((BLK, BLK, CH), bf16),
            jax.ShapeDtypeStruct((CH, 5 * CH), f32),
            jax.ShapeDtypeStruct((8, CH), f32),
        ],
        scratch_shapes=[pltpu.VMEM((CH, 5 * CH), bf16)],
        name="back",
        compiler_params=pltpu.CompilerParams(vmem_limit_bytes=LIMIT),
    )(pm, gfa, gfb, a1, a2, b1, b2, gg, *vecs, *weights)


def peer(axis, d):
    return lax.rem(lax.axis_index(axis) + d, DEV)


def greet(axes):
    barrier = pltpu.get_barrier_semaphore()
    for axis in axes:

        def hello(d, carry):
            pl.semaphore_signal(
                barrier, inc=1, device_id={axis: peer(axis, d)}, device_id_type=MESH
            )
            return carry

        lax.fori_loop(1, DEV, hello, 0)
    pl.semaphore_wait(barrier, len(axes) * (DEV - 1))


def each(action):
    def run(d, carry):
        action(d)
        return carry

    lax.fori_loop(1, DEV, run, 0)


def copier(axis, src, dst, send, recv):
    def make(d):
        t = peer(axis, d)
        return pltpu.make_async_remote_copy(
            src_ref=src(t),
            dst_ref=dst,
            send_sem=send.at[d],
            recv_sem=recv.at[d],
            device_id={axis: t},
            device_id_type=MESH,
        )

    return make


def span(count, action, start=0):
    def run(d, carry):
        action(d)
        return carry

    lax.fori_loop(start, count, run, 0)


def arrive(ref, sem):
    pltpu.make_async_copy(ref, ref, sem).wait()


def push(src, dst, send, recv, axis, t):
    pltpu.make_async_remote_copy(
        src_ref=src,
        dst_ref=dst,
        send_sem=send,
        recv_sem=recv,
        device_id={axis: t},
        device_id_type=MESH,
    ).start()


def keep(src, dst, sem):
    pltpu.make_async_copy(src, dst, sem).start()


def assemble(src, scr, dst, first):
    for a in range(PACK):
        rows = jnp.concatenate(
            [src[q][:, a * BLK : (a + 1) * BLK].astype(f32) for q in range(DEV)], axis=1
        )
        for t in range(NT):
            scr[t, pl.ds(a, CPROWS, stride=PACK), :] = rows[:, t * 128 : (t + 1) * 128]
    for t in range(NT):
        dst[first : first + PN, t * 128 : (t + 1) * 128] = scr[t].astype(bf16)


def turn_order():
    lane = lax.broadcasted_iota(jnp.int32, (N, N), 1)
    sub = lax.broadcasted_iota(jnp.int32, (N, N), 0)
    piece = lane >> 8
    place = ((lane >> 4) & 15) * BLK + piece * STEP + (lane & 15)
    return jnp.where(place == sub, 1.0, 0.0).astype(bf16)


def tri_kernel(
    gx, fa, fb, ga, gb,
    rbuf, scr, sbuf, gq, fq, asm, gn, left, order, fn, acc, dis, cbuf, hbuf,
    r_send, r_recv, g_send, g_recv, x_send, x_recv, f_send, f_recv,
    c_send, c_recv, h_send, h_recv,
):
    row, col = lax.axis_index("row"), lax.axis_index("col")
    odd = lax.rem(col, 2)
    sibling = col + 1 - 2 * odd
    arrays = (gx, fb, fa)
    outs = (ga, gb)
    greet(("row", "col"))
    for a in range(3):
        for p in range(NSTEP):
            keep(arrays[a].at[p, row], rbuf.at[a, p, row], r_recv.at[a, p])

            def send(d, a=a, p=p):
                t = peer("row", d)
                push(
                    arrays[a].at[p, t], rbuf.at[a, p, row], r_send.at[a], r_recv.at[a, p], "row", t
                )

            span(DEV, send, 1)
    order[...] = turn_order()

    def shuffle(a, p):
        arrive(rbuf.at[a, p], r_recv.at[a, p])
        for t in range(TILES):
            lanes = slice(t * 128, (t + 1) * 128)
            scr[t] = rbuf[a, p, :, :, lanes].reshape(DEV * PROWS, 128).astype(f32)
            for m in range(CPD):
                sbuf[a, p, m, :, lanes] = scr[t, pl.ds(m, CPROWS, stride=CPD), :].astype(bf16)

    HALF = CPROWS // 2

    def half(h):
        return pl.ds(pl.multiple_of(h * HALF, HALF), HALF)

    for p in range(NSTEP):
        shuffle(0, p)
        keep(sbuf.at[0, p, col // 2, half(odd)], gq.at[p, col, half(odd)], g_recv.at[p])

        def send(d, p=p):
            t = peer("col", d)
            h = half(lax.rem(t, 2))
            push(sbuf.at[0, p, t // 2, h], gq.at[p, col, h], g_send, g_recv.at[p], "col", t)

        span(DEV, send, 1)

    def factor(a, p):
        shuffle(a, p)
        same = odd == a - 1

        @pl.when(same)
        def _():
            keep(sbuf.at[a, p, col // 2], fq.at[p, col], f_recv.at[p])

        def send(d):
            t = lax.rem(col + 2 * d + jnp.where(same, 0, 1), DEV)
            push(sbuf.at[a, p, t // 2], fq.at[p, col], f_send, f_recv.at[p], "col", t)

        span(DEV // 2, send, jnp.where(same, 1, 0))

    factor(1, 0)
    for p in range(NSTEP):
        arrive(gq.at[p, :, half(odd)], g_recv.at[p])
        push(
            gq.at[p, :, half(odd)],
            gq.at[p, :, half(odd)],
            x_send.at[p],
            x_recv.at[p],
            "col",
            sibling,
        )
    factor(1, 1)
    factor(1, 2)
    for p in range(NSTEP):
        arrive(gq.at[p, :, half(1 - odd)], x_recv.at[p])
        assemble(gq.at[p], asm, gn, p * PN)

    @pl.when(odd == 0)
    def _():
        left[...] = dot(gn[...], order[...]).astype(bf16)

    @pl.when(odd == 1)
    def _():
        left[...] = dot(order[...], gn[...], 0, 1).astype(bf16)

    factor(2, 0)

    def multiply():
        for p in range(NSTEP):
            arrive(fq.at[p], f_recv.at[p])
            assemble(fq.at[p], asm, fn, 0)
            values = dot(left[:, p * PN : (p + 1) * PN], fn[...])
            for t in range(NT):
                lanes = values[:, t * 128 : (t + 1) * 128]
                if p == 0:
                    acc[t] = lanes
                else:
                    acc[t] += lanes
        for p in range(NSTEP):
            rows = [
                [acc[t, pl.ds(p * PN + a, CPROWS, stride=PACK), :] for t in range(NT)]
                for a in range(PACK)
            ]

            def piece(a, q):
                lo, hi = q * BLK, (q + 1) * BLK
                first, last = lo // 128, (hi - 1) // 128
                if first == last:
                    return rows[a][first][:, lo - first * 128 : hi - first * 128]
                return jnp.concatenate(
                    [rows[a][first][:, lo - first * 128 :], rows[a][last][:, : hi - last * 128]],
                    axis=1,
                )

            for q in range(DEV):
                dis[p, q] = jnp.concatenate([piece(a, q) for a in range(PACK)], axis=1).astype(bf16)
            keep(dis.at[p, col], cbuf.at[p, col], c_recv.at[odd, p])

            def send(d):
                t = peer("col", d)
                push(dis.at[p, t], cbuf.at[p, col], c_send, c_recv.at[odd, p], "col", t)

            span(DEV, send, 1)

    pl.when(odd == 0)(multiply)
    factor(2, 1)
    factor(2, 2)
    pl.when(odd == 1)(multiply)

    for h in range(2):
        for p in range(NSTEP):
            arrive(cbuf.at[p, 0 : DEV // 2], c_recv.at[h, p])
            for t in range(TILES):
                lanes = slice(t * 128, (t + 1) * 128)
                for m in range(CPD):
                    scr[t, pl.ds(m, CPROWS, stride=CPD), :] = cbuf[p, 2 * m + h, :, lanes].astype(
                        f32
                    )
                hbuf[h, p, :, :, lanes] = scr[t].reshape(DEV, PROWS, 128).astype(bf16)
            keep(hbuf.at[h, p, row], outs[h].at[p, row], h_recv.at[h, p])

            def send(d, h=h, p=p):
                t = peer("row", d)
                push(hbuf.at[h, p, t], outs[h].at[p, row], h_send, h_recv.at[h, p], "row", t)

            span(DEV, send, 1)

    for h in range(2):
        for p in range(NSTEP):
            arrive(outs[h].at[p], h_recv.at[h, p])
    for a in range(3):
        arrive(rbuf.at[a, :, 0 : DEV - 1], r_send.at[a])
    arrive(gq.at[:, 0 : DEV - 1, 0:HALF], g_send)
    for p in range(NSTEP):
        arrive(gq.at[p, :, 0:HALF], x_send.at[p])
    arrive(fq.at[:, 0 : DEV - 1], f_send)
    arrive(cbuf.at[:, 0 : DEV - 1], c_send)
    arrive(hbuf.at[:, :, 0 : DEV - 1], h_send)


def tri(gx, fa, fb):
    dma = pltpu.SemaphoreType.DMA
    turned = (NSTEP, DEV, PROWS, LANES)
    crossed = (NSTEP, DEV, CPROWS, LANES)
    return pl.pallas_call(
        tri_kernel,
        in_specs=[VMEM] * 3,
        out_specs=[VMEM] * 2,
        out_shape=[TURNED] * 2,
        scratch_shapes=[
            pltpu.VMEM((3,) + turned, bf16),
            pltpu.VMEM((TILES, DEV * PROWS, 128), f32),
            pltpu.VMEM((3, NSTEP, CPD, CPROWS, LANES), bf16),
            pltpu.VMEM(crossed, bf16),
            pltpu.VMEM(crossed, bf16),
            pltpu.VMEM((NT, PN, 128), f32),
            pltpu.VMEM((N, N), bf16),
            pltpu.VMEM((N, N), bf16),
            pltpu.VMEM((N, N), bf16),
            pltpu.VMEM((PN, N), bf16),
            pltpu.VMEM((NT, N, 128), f32),
            pltpu.VMEM(crossed, bf16),
            pltpu.VMEM(crossed, bf16),
            pltpu.VMEM((2,) + turned, bf16),
            dma((3,)),
            dma((3, NSTEP)),
            dma,
            dma((NSTEP,)),
            dma((NSTEP,)),
            dma((NSTEP,)),
            dma,
            dma((NSTEP,)),
            dma,
            dma((2, NSTEP)),
            dma,
            dma((2, NSTEP)),
        ],
        name="tri",
        compiler_params=pltpu.CompilerParams(
            collective_id=1, has_side_effects=True, vmem_limit_bytes=LIMIT
        ),
    )(gx, fa, fb)


def sum_kernel(gw, gwo, gvec, lvec, out, part, got1, mid, got2, fin, sem_s, sem_r, loc):
    row, col = lax.axis_index("row"), lax.axis_index("col")
    for k in range(5):
        for j in range(2):
            part[2 * k + j] = gw[j * 64 : (j + 1) * 64, k * CH : (k + 1) * CH].astype(bf16)
    for j in range(2):
        part[10 + j] = gwo[j * 64 : (j + 1) * 64, :].astype(bf16)
    part[12] = jnp.concatenate(
        [lvec[...], gvec[...], jnp.zeros((SUMROWS - 16, CH), f32)], axis=0
    ).astype(bf16)
    part[13:16] = jnp.zeros((3, SUMROWS, CH), bf16)
    own = pltpu.make_async_copy(part.at[col], got1.at[col], loc.at[0])
    own.start()
    greet(("row", "col"))
    one = copier("col", lambda t: part.at[t], got1.at[col], sem_s.at[0], sem_r.at[0])
    each(lambda d: one(d).start())
    own.wait()
    each(lambda d: one(d).wait())
    mid[...] = jnp.sum(got1[...].astype(f32), axis=0).astype(bf16)
    own = pltpu.make_async_copy(mid, got2.at[row], loc.at[1])
    own.start()
    two = copier("row", lambda t: mid, got2.at[row], sem_s.at[1], sem_r.at[1])
    each(lambda d: two(d).start())
    own.wait()
    each(lambda d: two(d).wait())
    fin[...] = (jnp.sum(got2[...].astype(f32), axis=0) * (1.0 / N)).astype(bf16)
    own = pltpu.make_async_copy(fin, out.at[col], loc.at[2])
    own.start()
    three = copier("col", lambda t: fin, out.at[col], sem_s.at[2], sem_r.at[2])
    each(lambda d: three(d).start())
    own.wait()
    each(lambda d: three(d).wait())


def sum_all(gw, gwo, gvec, lvec):
    dma = pltpu.SemaphoreType.DMA
    wide = (DEV, SUMROWS, CH)
    return pl.pallas_call(
        sum_kernel,
        in_specs=[VMEM] * 4,
        out_specs=VMEM,
        out_shape=jax.ShapeDtypeStruct(wide, bf16),
        scratch_shapes=[
            pltpu.VMEM(wide, bf16),
            pltpu.VMEM(wide, bf16),
            pltpu.VMEM((SUMROWS, CH), bf16),
            pltpu.VMEM(wide, bf16),
            pltpu.VMEM((SUMROWS, CH), bf16),
            dma((3, DEV)),
            dma((3, DEV)),
            dma((3,)),
        ],
        name="sum_all",
        compiler_params=pltpu.CompilerParams(
            collective_id=3, has_side_effects=True, vmem_limit_bytes=LIMIT
        ),
    )(gw, gwo, gvec, lvec)


def finish_kernel(s, *outs):
    for k in range(6):
        for j in range(2):
            outs[k][j * 64 : (j + 1) * 64, :] = s[2 * k + j].astype(f32)
    vec = s[12].astype(f32)
    outs[6][...] = vec[0:1]
    outs[7][...] = vec[1:2]
    outs[8][...] = vec[8:9]
    outs[9][...] = vec[9:10]


def finish(s):
    return pl.pallas_call(
        finish_kernel,
        in_specs=[VMEM],
        out_specs=[VMEM] * 10,
        out_shape=[jax.ShapeDtypeStruct((CH, CH), f32)] * 6
        + [jax.ShapeDtypeStruct((1, CH), f32)] * 4,
        name="finish",
    )(s)


def body(
    pair_map,
    saved_product,
    cotangent,
    residue_mask,
    ln_gain,
    ln_bias,
    out_gain,
    out_bias,
    w_a,
    w_ag,
    w_b,
    w_bg,
    w_g,
    w_o,
):
    vecs = [v.reshape(1, CH) for v in (ln_gain, ln_bias, out_gain, out_bias)]
    weights = [w_a, w_ag, w_b, w_bg, w_g, w_o]
    gx, fa, fb, a1, a2, b1, b2, gg, gwo, gvec = front(
        pair_map, saved_product, cotangent, residue_mask.reshape(1, N), vecs, weights
    )
    gfa, gfb = tri(gx, fa, fb)
    grad_pair, gw, lvec = back(
        pair_map, gfa, gfb, a1, a2, b1, b2, gg, vecs[:2], weights[:5]
    )
    outs = finish(sum_all(gw, gwo, gvec, lvec))
    return (grad_pair,) + tuple(outs[:6]) + tuple(v.reshape(CH) for v in outs[6:])


def solution(mesh):
    return jax.shard_map(
        body,
        mesh=mesh,
        in_specs=(P("row", "col", None),) * 3 + (P(),) * 11,
        out_specs=(P("row", "col", None),) + (P(),) * 10,
        check_vma=False,
    )
```

```python
import jax
import jax.numpy as jnp
from jax import lax
from jax.experimental import pallas as pl
from jax.experimental.pallas import tpu as pltpu
from jax.sharding import PartitionSpec as P

MESH = pl.DeviceIdType.MESH
f32 = jnp.float32
bf16 = jnp.bfloat16
epsilon = 1e-05
VMEM = pl.BlockSpec(memory_space=pltpu.VMEM)
LIMIT = 56 << 20

DEV = 16
BLK = 48
CH = 128
PACK = 8
GROUPS = BLK // PACK
LANES = PACK * BLK
TILES = LANES // 128
CPD = CH // DEV
ROWS = GROUPS * CPD
CROWS = GROUPS * DEV
N = DEV * BLK
STEP = 16
CELLS = STEP * BLK
NSTEP = BLK // STEP
EARLY = 4 * CH // DEV
LATE = 2 * CH // DEV
PROWS = STEP // PACK * CPD
CPROWS = STEP // PACK * DEV
PN = STEP * DEV
NT = N // 128
ODD = 11


def dot(a, b, ca=1, cb=0):
    return lax.dot_general(a, b, (((ca,), (cb,)), ((), ())), preferred_element_type=f32)


def mean(v):
    return jnp.mean(v, axis=-1, keepdims=True)


def normalize(values):
    values = values.astype(f32)
    centred = values - mean(values)
    inverse = lax.rsqrt(mean(centred * centred) + epsilon)
    return centred * inverse, inverse


def norm_back(scaled, normed, inverse):
    return inverse * (scaled - mean(scaled) - normed * mean(scaled * normed))


def to_channels(ref, values):
    halves = []
    for g in range(STEP // PACK):
        turned = values[g * LANES : (g + 1) * LANES].T
        halves.append(turned.reshape(DEV, CPD, LANES))
    ref[...] = jnp.concatenate(halves, axis=1).astype(bf16)


def from_channels(ref):
    values = ref[...].astype(f32)
    parts = []
    for g in range(STEP // PACK):
        parts.append(values[:, g * CPD : (g + 1) * CPD, :].reshape(CH, LANES).T)
    return jnp.concatenate(parts, axis=0)


def add_to(ref, values, first):
    if first:
        ref[...] = values
    else:
        ref[...] += values


def column_sum(values):
    return jnp.sum(values, axis=0, keepdims=True)


def mask_of(rmask, axis):
    first = lax.axis_index(axis) * BLK
    lane = lax.broadcasted_iota(jnp.int32, (BLK, N), 1)
    sub = lax.broadcasted_iota(jnp.int32, (BLK, N), 0)
    picked = jnp.where(lane == sub + first, rmask[...].astype(f32), 0.0)
    return jnp.broadcast_to(jnp.sum(picked, axis=1, keepdims=True), (BLK, CH))


def peer(axis, d):
    return lax.axis_index(axis) ^ d


def span(count, action, start=0):
    def run(d, carry):
        action(d)
        return carry

    lax.fori_loop(start, count, run, 0)


def arrive(ref, sem):
    pltpu.make_async_copy(ref, ref, sem).wait()


def push(src, dst, send, recv, axis, t):
    pltpu.make_async_remote_copy(
        src_ref=src,
        dst_ref=dst,
        send_sem=send,
        recv_sem=recv,
        device_id={axis: t},
        device_id_type=MESH,
    ).start()


def keep(src, dst, sem):
    pltpu.make_async_copy(src, dst, sem).start()


def scatter(axis, src, dst, send, recv):
    me = lax.axis_index(axis)
    keep(src(me), dst.at[me], recv)

    def go(d):
        t = peer(axis, (d * ODD) & (DEV - 1))
        push(src(t), dst.at[me], send, recv, axis, t)

    span(DEV, go, 1)


def assemble(src, scr, dst, first):
    for a in range(PACK):
        rows = jnp.concatenate(
            [src[q][:, a * BLK : (a + 1) * BLK].astype(f32) for q in range(DEV)], axis=1
        )
        for t in range(NT):
            scr[t, pl.ds(a, CPROWS, stride=PACK), :] = rows[:, t * 128 : (t + 1) * 128]
    for t in range(NT):
        dst[first : first + PN, t * 128 : (t + 1) * 128] = scr[t].astype(bf16)


def turn_order():
    lane = lax.broadcasted_iota(jnp.int32, (N, N), 1)
    sub = lax.broadcasted_iota(jnp.int32, (N, N), 0)
    piece = lane >> 8
    place = ((lane >> 4) & 15) * BLK + piece * STEP + (lane & 15)
    return jnp.where(place == sub, 1.0, 0.0).astype(bf16)


def kernel(
    pm, sp, ct, rmask, lg, lb, og, ob, wa, wag, wb, wbg, wg, wo,
    gp, eout, lout, vout,
    zn, hat, inv, a1, a2, b1, b2, gg, gz, gwo, gwa, gwb, lvec, wcat, tx, rx,
    rbuf, scr, sbuf, gq, fq, asm, gn, left, order, fn, acc, dis, cbuf, hbuf,
    epart, eg1, emid, eg2, efin, lpart, lg1, lmid, lg2, lfin,
    r_send, r_recv, g_send, g_recv, x_send, x_recv, f_send, f_recv,
    c_send, c_recv, h_send, h_recv, e_send, e_recv, l_send, l_recv,
):
    row, col = lax.axis_index("row"), lax.axis_index("col")
    odd = lax.rem(col, 2)
    sibling = col + 1 - 2 * odd
    barrier = pltpu.get_barrier_semaphore()
    for axis in ("row", "col"):

        def hello(d, axis=axis):
            pl.semaphore_signal(
                barrier, inc=1, device_id={axis: peer(axis, d)}, device_id_type=MESH
            )

        span(DEV, hello, 1)

    lvec[...] = jnp.zeros((8, CH), f32)
    rm = mask_of(rmask, "row")
    km = mask_of(rmask, "col")
    for k, w in enumerate((wa, wag, wg, wb, wbg)):
        wcat[:, k * CH : (k + 1) * CH] = w[...]

    def cells(p):
        return slice(p * CELLS, (p + 1) * CELLS)

    def rows_of(p):
        return slice(p * STEP, (p + 1) * STEP)

    def launch(a, p):
        scatter("row", lambda t: tx.at[a, p, t], rbuf.at[a, p], r_send.at[a], r_recv.at[a, p])

    for p in range(NSTEP):
        here = cells(p)
        phat, pinv = normalize(pm[rows_of(p)].reshape(CELLS, CH))
        hat[here] = phat
        inv[here] = jnp.broadcast_to(pinv, (CELLS, CH))
        znp = (phat * lg[...] + lb[...]).astype(bf16)
        zn[here] = znp
        ohat, oinv = normalize(sp[rows_of(p)].reshape(CELLS, CH))
        xn = (ohat * og[...] + ob[...]).astype(bf16)
        gate = jax.nn.sigmoid(dot(znp, wg[...]))
        up = ct[rows_of(p)].reshape(CELLS, CH).astype(f32) * gate
        gu = up.astype(bf16)
        gxn = dot(gu, wo[...], 1, 1)
        to_channels(tx.at[0, p], norm_back(gxn * og[...], ohat, oinv))
        if p == 0:
            pl.semaphore_wait(barrier, 2 * (DEV - 1))
        launch(0, p)
        update = dot(xn, wo[...])
        gg[here] = (up * update * (1.0 - gate)).astype(bf16)
        add_to(gwo, dot(xn, gu, 0, 0), p == 0)
        add_to(lvec.at[2:3], column_sum(gxn * ohat), p == 0)
        add_to(lvec.at[3:4], column_sum(gxn), p == 0)

    for a, w, wgate, k1, k2 in ((1, wb, wbg, b1, b2), (2, wa, wag, a1, a2)):
        for p in range(NSTEP):
            here = cells(p)
            mask = jnp.broadcast_to(
                rm[rows_of(p)][:, None, :] * km[None], (STEP, BLK, CH)
            ).reshape(CELLS, CH)
            sig = jax.nn.sigmoid(dot(zn[here], wgate[...]))
            masked = mask * sig
            fac = masked * dot(zn[here], w[...])
            to_channels(tx.at[a, p], fac)
            launch(a, p)
            k1[here] = masked
            k2[here] = fac * (1.0 - sig)
    order[...] = turn_order()

    def shuffle(a, p):
        arrive(rbuf.at[a, p], r_recv.at[a, p])
        for t in range(TILES):
            lanes = slice(t * 128, (t + 1) * 128)
            scr[t] = rbuf[a, p, :, :, lanes].reshape(DEV * PROWS, 128).astype(f32)
            for m in range(CPD):
                sbuf[a, p, m, :, lanes] = scr[t, pl.ds(m, CPROWS, stride=CPD), :].astype(bf16)

    HALF = CPROWS // 2

    def half(h):
        return pl.ds(pl.multiple_of(h * HALF, HALF), HALF)

    for p in range(NSTEP):
        shuffle(0, p)
        keep(sbuf.at[0, p, col // 2, half(odd)], gq.at[p, col, half(odd)], g_recv.at[p])

        def send(d, p=p):
            t = peer("col", (d * ODD) & (DEV - 1))
            h = half(lax.rem(t, 2))
            push(sbuf.at[0, p, t // 2, h], gq.at[p, col, h], g_send, g_recv.at[p], "col", t)

        span(DEV, send, 1)

    def factor(a, p):
        shuffle(a, p)
        same = odd == a - 1

        @pl.when(same)
        def _():
            keep(sbuf.at[a, p, col // 2], fq.at[p, col], f_recv.at[p])

        def send(d):
            t = col ^ (2 * ((d * ODD) & (DEV // 2 - 1)) + jnp.where(same, 0, 1))
            push(sbuf.at[a, p, t // 2], fq.at[p, col], f_send, f_recv.at[p], "col", t)

        span(DEV // 2, send, jnp.where(same, 1, 0))

    factor(1, 0)
    for p in range(NSTEP):
        arrive(gq.at[p, :, half(odd)], g_recv.at[p])
        push(
            gq.at[p, :, half(odd)],
            gq.at[p, :, half(odd)],
            x_send.at[p],
            x_recv.at[p],
            "col",
            sibling,
        )
    factor(1, 1)
    factor(1, 2)
    for p in range(NSTEP):
        arrive(gq.at[p, :, half(1 - odd)], x_recv.at[p])
        assemble(gq.at[p], asm, gn, p * PN)

    @pl.when(odd == 0)
    def _():
        left[...] = dot(gn[...], order[...]).astype(bf16)

    @pl.when(odd == 1)
    def _():
        left[...] = dot(order[...], gn[...], 0, 1).astype(bf16)

    factor(2, 0)

    def multiply():
        for p in range(NSTEP):
            arrive(fq.at[p], f_recv.at[p])
            assemble(fq.at[p], asm, fn, 0)
            values = dot(left[:, p * PN : (p + 1) * PN], fn[...])
            for t in range(NT):
                lanes = values[:, t * 128 : (t + 1) * 128]
                if p == 0:
                    acc[t] = lanes
                else:
                    acc[t] += lanes
        for p in range(NSTEP):
            rows = [
                [acc[t, pl.ds(p * PN + a, CPROWS, stride=PACK), :] for t in range(NT)]
                for a in range(PACK)
            ]

            def piece(a, q):
                lo, hi = q * BLK, (q + 1) * BLK
                first, last = lo // 128, (hi - 1) // 128
                if first == last:
                    return rows[a][first][:, lo - first * 128 : hi - first * 128]
                return jnp.concatenate(
                    [rows[a][first][:, lo - first * 128 :], rows[a][last][:, : hi - last * 128]],
                    axis=1,
                )

            for q in range(DEV):
                dis[p, q] = jnp.concatenate([piece(a, q) for a in range(PACK)], axis=1).astype(bf16)
            scatter("col", lambda t: dis.at[p, t], cbuf.at[p], c_send, c_recv.at[odd, p])

    pl.when(odd == 0)(multiply)
    factor(2, 1)
    factor(2, 2)
    pl.when(odd == 1)(multiply)

    def relay(h, p):
        arrive(cbuf.at[p, 0 : DEV // 2], c_recv.at[h, p])
        for t in range(TILES):
            lanes = slice(t * 128, (t + 1) * 128)
            for m in range(CPD):
                scr[t, pl.ds(m, CPROWS, stride=CPD), :] = cbuf[p, 2 * m + h, :, lanes].astype(f32)
            hbuf[h, p, :, :, lanes] = scr[t].reshape(DEV, PROWS, 128).astype(bf16)
        scatter("row", lambda t: hbuf.at[h, p, t], rx.at[h, p], h_send, h_recv.at[h, p])

    for h in range(2):
        for p in range(NSTEP):
            relay(h, p)

    def grads_of(h, p, k1, k2):
        arrive(rx.at[h, p], h_recv.at[h, p])
        got = from_channels(rx.at[h, p])
        here = cells(p)
        return [(got * k1[here]).astype(bf16), (got * k2[here]).astype(bf16)]

    for p in range(NSTEP):
        here = cells(p)
        grads = jnp.concatenate(grads_of(0, p, a1, a2) + [gg[here]], axis=1)
        gz[here] = dot(grads, wcat[:, : 3 * CH], 1, 1)
        add_to(gwa, dot(zn[here], grads, 0, 0), p == 0)

    for t in range(DEV):
        k, at = divmod(t * EARLY, CH)
        source = gwo[at : at + EARLY, :] if k == 3 else gwa[at : at + EARLY, k * CH : (k + 1) * CH]
        epart[t] = source.astype(bf16)
    scatter("col", lambda t: epart.at[t], eg1, e_send.at[0], e_recv.at[0])

    def last(p):
        here = cells(p)
        grads = jnp.concatenate(grads_of(1, p, b1, b2), axis=1)
        total = gz[here] + dot(grads, wcat[:, 3 * CH :], 1, 1)
        add_to(gwb, dot(zn[here], grads, 0, 0), p == 0)
        add_to(lvec.at[0:1], column_sum(total * hat[here]), p == 0)
        add_to(lvec.at[1:2], column_sum(total), p == 0)
        return total

    def write(p, total):
        here = cells(p)
        value = norm_back(total * lg[...], hat[here], inv[here])
        gp[rows_of(p)] = value.astype(bf16).reshape(STEP, BLK, CH)

    write(0, last(0))
    arrive(eg1, e_recv.at[0])
    emid[...] = jnp.sum(eg1[...].astype(f32), axis=0).astype(bf16)
    scatter("row", lambda t: emid, eg2, e_send.at[1], e_recv.at[1])
    write(1, last(1))
    arrive(eg2, e_recv.at[1])
    efin[...] = (jnp.sum(eg2[...].astype(f32), axis=0) * (1.0 / N)).astype(bf16)
    scatter("col", lambda t: efin, eout, e_send.at[2], e_recv.at[2])
    total = last(2)

    vector = jnp.concatenate([lvec[...], jnp.zeros((8, CH), f32)], axis=0)
    for t in range(DEV):
        k, at = divmod(t * LATE, CH)
        source = gwb[at : at + LATE, k * CH : (k + 1) * CH]
        lpart[t] = jnp.concatenate([source, vector], axis=0).astype(bf16)
    scatter("col", lambda t: lpart.at[t], lg1, l_send.at[0], l_recv.at[0])
    write(2, total)
    arrive(lg1, l_recv.at[0])
    lmid[...] = jnp.sum(lg1[...].astype(f32), axis=0).astype(bf16)
    scatter("row", lambda t: lmid, lg2, l_send.at[1], l_recv.at[1])
    arrive(lg2, l_recv.at[1])
    done = jnp.sum(lg2[...].astype(f32), axis=0) * (1.0 / N)
    vout[...] = done[LATE:]
    lfin[...] = done[:LATE].astype(bf16)
    scatter("col", lambda t: lfin, lout, l_send.at[2], l_recv.at[2])

    for a in range(3):
        arrive(rbuf.at[a, :, 0 : DEV - 1], r_send.at[a])
    arrive(gq.at[:, 0 : DEV - 1, 0:HALF], g_send)
    for p in range(NSTEP):
        arrive(gq.at[p, :, 0:HALF], x_send.at[p])
    arrive(fq.at[:, 0 : DEV - 1], f_send)
    arrive(cbuf.at[:, 0 : DEV - 1], c_send)
    arrive(hbuf.at[:, :, 0 : DEV - 1], h_send)
    for k in range(3):
        arrive(eg1.at[0 : DEV - 1], e_send.at[k])
    arrive(lg1.at[0 : DEV - 1], l_send.at[0])
    arrive(lg2.at[0 : DEV - 1], l_send.at[1])
    arrive(lout.at[0 : DEV - 1], l_send.at[2])
    arrive(eout, e_recv.at[2])
    arrive(lout, l_recv.at[2])


def whole_step(*args):
    dma = pltpu.SemaphoreType.DMA
    turned = (NSTEP, DEV, PROWS, LANES)
    crossed = (NSTEP, DEV, CPROWS, LANES)
    flat = (BLK * BLK, CH)
    early = (DEV, EARLY, CH)
    late = (DEV, LATE + 16, CH)

    def wide(*shape):
        return pltpu.VMEM(shape, f32)

    def thin(*shape):
        return pltpu.VMEM(shape, bf16)

    return pl.pallas_call(
        kernel,
        in_specs=[VMEM] * 14,
        out_specs=[VMEM] * 4,
        out_shape=[
            jax.ShapeDtypeStruct((BLK, BLK, CH), bf16),
            jax.ShapeDtypeStruct(early, bf16),
            jax.ShapeDtypeStruct((DEV, LATE, CH), bf16),
            jax.ShapeDtypeStruct((16, CH), f32),
        ],
        scratch_shapes=[
            thin(*flat),
            wide(*flat),
            wide(*flat),
            wide(*flat),
            wide(*flat),
            wide(*flat),
            wide(*flat),
            thin(*flat),
            wide(*flat),
            wide(CH, CH),
            wide(CH, 3 * CH),
            wide(CH, 2 * CH),
            wide(8, CH),
            thin(CH, 5 * CH),
            thin(3, *turned),
            thin(2, *turned),
            thin(3, *turned),
            wide(TILES, DEV * PROWS, 128),
            thin(3, NSTEP, CPD, CPROWS, LANES),
            thin(*crossed),
            thin(*crossed),
            wide(NT, PN, 128),
            thin(N, N),
            thin(N, N),
            thin(N, N),
            thin(PN, N),
            wide(NT, N, 128),
            thin(*crossed),
            thin(*crossed),
            thin(2, *turned),
            thin(*early),
            thin(*early),
            thin(EARLY, CH),
            thin(*early),
            thin(EARLY, CH),
            thin(*late),
            thin(*late),
            thin(LATE + 16, CH),
            thin(*late),
            thin(LATE, CH),
            dma((3,)),
            dma((3, NSTEP)),
            dma,
            dma((NSTEP,)),
            dma((NSTEP,)),
            dma((NSTEP,)),
            dma,
            dma((NSTEP,)),
            dma,
            dma((2, NSTEP)),
            dma,
            dma((2, NSTEP)),
            dma((3,)),
            dma((3,)),
            dma((3,)),
            dma((3,)),
        ],
        name="whole_step",
        compiler_params=pltpu.CompilerParams(
            collective_id=1, has_side_effects=True, vmem_limit_bytes=LIMIT
        ),
    )(*args)


def finish_kernel(pair, early, late, vec, *outs):
    outs[0][...] = pair[...]
    place = (1, 2, 5, 6)
    for t in range(DEV):
        k, at = divmod(t * EARLY, CH)
        outs[place[k]][at : at + EARLY, :] = early[t].astype(f32)
        k, at = divmod(t * LATE, CH)
        outs[3 + k][at : at + LATE, :] = late[t].astype(f32)
    for k in range(4):
        outs[7 + k][...] = vec[k : k + 1]


def finish(*args):
    return pl.pallas_call(
        finish_kernel,
        in_specs=[VMEM] * 4,
        out_specs=[VMEM] * 11,
        out_shape=[jax.ShapeDtypeStruct((BLK, BLK, CH), bf16)]
        + [jax.ShapeDtypeStruct((CH, CH), f32)] * 6
        + [jax.ShapeDtypeStruct((1, CH), f32)] * 4,
        name="finish",
    )(*args)


def body(
    pair_map,
    saved_product,
    cotangent,
    residue_mask,
    ln_gain,
    ln_bias,
    out_gain,
    out_bias,
    *weights,
):
    vecs = [v.reshape(1, CH) for v in (ln_gain, ln_bias, out_gain, out_bias)]
    outs = finish(
        *whole_step(
            pair_map, saved_product, cotangent, residue_mask.reshape(1, N), *vecs, *weights
        )
    )
    return tuple(outs[:7]) + tuple(v.reshape(CH) for v in outs[7:])


def solution(mesh):
    return jax.shard_map(
        body,
        mesh=mesh,
        in_specs=(P("row", "col", None),) * 3 + (P(),) * 11,
        out_specs=(P("row", "col", None),) + (P(),) * 10,
        check_vma=False,
    )
```

```python
import jax
import jax.numpy as jnp
from jax import lax
from jax.experimental import pallas as pl
from jax.experimental.pallas import tpu as pltpu
from jax.sharding import PartitionSpec as P

MESH = pl.DeviceIdType.MESH
f32 = jnp.float32
bf16 = jnp.bfloat16
epsilon = 1e-05
VMEM = pl.BlockSpec(memory_space=pltpu.VMEM)
LIMIT = 56 << 20

DEV = 16
BLK = 48
CH = 128
PACK = 8
LANES = PACK * BLK
TILES = LANES // 128
ZN = 8
PLANE = 32
CPZ = CH // ZN
N = DEV * BLK
STEP = 16
CELLS = STEP * BLK
NSTEP = BLK // STEP
EARLY = 4 * CH // DEV
LATE = 2 * CH // DEV
PROWS = STEP // PACK * CPZ
CPROWS = STEP // PACK * ZN
PN = STEP * DEV
NT = N // 128


def dot(a, b, ca=1, cb=0):
    return lax.dot_general(a, b, (((ca,), (cb,)), ((), ())), preferred_element_type=f32)


def mean(v):
    return jnp.mean(v, axis=-1, keepdims=True)


def normalize(values):
    values = values.astype(f32)
    centred = values - mean(values)
    inverse = lax.rsqrt(mean(centred * centred) + epsilon)
    return centred * inverse, inverse


def norm_back(scaled, normed, inverse):
    return inverse * (scaled - mean(scaled) - normed * mean(scaled * normed))


def to_channels(ref, values):
    halves = []
    for g in range(STEP // PACK):
        turned = values[g * LANES : (g + 1) * LANES].T
        halves.append(turned.reshape(ZN, CPZ, LANES))
    ref[...] = jnp.concatenate(halves, axis=1).astype(bf16)


def from_channels(ref):
    values = ref[...].astype(f32)
    parts = []
    for g in range(STEP // PACK):
        parts.append(values[:, g * CPZ : (g + 1) * CPZ, :].reshape(CH, LANES).T)
    return jnp.concatenate(parts, axis=0)


def add_to(ref, values, first):
    if first:
        ref[...] = values
    else:
        ref[...] += values


def column_sum(values):
    return jnp.sum(values, axis=0, keepdims=True)


def mask_of(rmask, axis):
    first = lax.axis_index(axis) * BLK
    lane = lax.broadcasted_iota(jnp.int32, (BLK, CH), 1)
    sub = lax.broadcasted_iota(jnp.int32, (BLK, CH), 0)
    picked = jnp.zeros((BLK, CH), f32)
    for t in range(NT):
        here = lane + t * CH == sub + first
        picked += jnp.where(here, rmask[t : t + 1, :].astype(f32), 0.0)
    return jnp.broadcast_to(jnp.sum(picked, axis=1, keepdims=True), (BLK, CH))


def peer(axis, d):
    return lax.axis_index(axis) ^ d


def span(count, action, start=0):
    def run(d, carry):
        action(d)
        return carry

    lax.fori_loop(start, count, run, 0)


def arrive(ref, sem):
    pltpu.make_async_copy(ref, ref, sem).wait()


def push(src, dst, send, recv, where):
    pltpu.make_async_remote_copy(
        src_ref=src,
        dst_ref=dst,
        send_sem=send,
        recv_sem=recv,
        device_id=where,
        device_id_type=MESH,
    ).start()


def keep(src, dst, sem):
    pltpu.make_async_copy(src, dst, sem).start()


def scatter_z(src, dst, send, recv):
    row = lax.axis_index("row")
    z = row >> 1
    keep(src(z), dst.at[z], recv)

    def go(d):
        k = ZN - d
        away = jnp.where((k & 1) == 1, (k + 1) >> 1, ZN - (k >> 1))
        t = (z + away) & (ZN - 1)
        push(src(t), dst.at[z], send, recv, {"row": 2 * t + (row & 1)})

    span(ZN, go, 1)


def scatter(axis, src, dst, send, recv):
    me = lax.axis_index(axis)
    keep(src(me), dst.at[me], recv)

    def go(d):
        t = peer(axis, DEV - d)
        push(src(t), dst.at[me], send, recv, {axis: t})

    span(DEV, go, 1)


def assemble(pick, scr, dst, first):
    for y in range(2):
        for a in range(PACK):
            rows = jnp.concatenate(
                [pick(y, q)[:, a * BLK : (a + 1) * BLK].astype(f32) for q in range(DEV)], axis=1
            )
            for t in range(NT):
                scr[t, pl.ds(y * (PN // 2) + a, CPROWS, stride=PACK), :] = rows[
                    :, t * 128 : (t + 1) * 128
                ]
    for t in range(NT):
        dst[first : first + PN, t * 128 : (t + 1) * 128] = scr[t].astype(bf16)


def turn_order():
    lane = lax.broadcasted_iota(jnp.int32, (N, N), 1)
    sub = lax.broadcasted_iota(jnp.int32, (N, N), 0)
    piece = lane >> 8
    device = 2 * ((lane >> 4) & 7) + ((lane >> 7) & 1)
    place = device * BLK + piece * STEP + (lane & 15)
    return jnp.where(place == sub, 1.0, 0.0).astype(bf16)


def kernel(
    *refs
):
    given, refs = refs[:14], refs[14:]
    (
        gp, eout, lout, vout,
        zn, hat, inv, a1, a2, b1, b2, gg, gz, gwo, gwa, gwb, lvec, wcat, tx, rx,
        rbuf, scr, sbuf, gq, fq, asm, gn, left, order, fn, acc, dis, cbuf, hbuf,
        epart, eg1, emid, eg2, efin, lpart, lg1, lmid, lg2, lfin,
        r_send, r_recv, g_send, g_recv, x_send, x_recv, f_send, f_recv,
        c_send, c_recv, h_send, h_recv, e_send, e_recv, l_send, l_recv, i_recv,
        *held
    ) = refs
    (
        pm, sp, ct, rmask, lg, lb, og, ob, wa, wag, wb, wbg, wg, wo,
    ) = held
    row, col = lax.axis_index("row"), lax.axis_index("col")
    odd = col & 1
    place = (row & 1) * DEV + col
    chip = place >> 1

    def at_place(t):
        return {"row": row - (row & 1) + (t >> 4), "col": t & (DEV - 1)}

    barrier = pltpu.get_barrier_semaphore()
    for axis in ("row", "col"):

        def hello(d, axis=axis):
            pl.semaphore_signal(
                barrier, inc=1, device_id={axis: peer(axis, d)}, device_id_type=MESH
            )

        span(DEV, hello, 1)

    def hello_plane(d):
        pl.semaphore_signal(
            barrier, inc=1, device_id={"row": row ^ 1, "col": col ^ d}, device_id_type=MESH
        )

    span(DEV, hello_plane, 1)

    for k in range(14):
        keep(given[k], held[k], i_recv.at[k])
    lvec[...] = jnp.zeros((8, CH), f32)
    for k in range(14):
        arrive(held[k], i_recv.at[k])
    rm = mask_of(rmask, "row")
    km = mask_of(rmask, "col")
    for k, w in enumerate((wa, wag, wg, wb, wbg)):
        wcat[:, k * CH : (k + 1) * CH] = w[...]

    def cells(p):
        return slice(p * CELLS, (p + 1) * CELLS)

    def rows_of(p):
        return slice(p * STEP, (p + 1) * STEP)

    def launch(a, p):
        scatter_z(lambda t: tx.at[a, p, t], rbuf.at[a, p], r_send.at[a], r_recv.at[a, p])

    for p in range(NSTEP):
        here = cells(p)
        phat, pinv = normalize(pm[rows_of(p)].reshape(CELLS, CH))
        hat[here] = phat
        inv[here] = jnp.broadcast_to(pinv, (CELLS, CH))
        znp = (phat * lg[...] + lb[...]).astype(bf16)
        zn[here] = znp
        ohat, oinv = normalize(sp[rows_of(p)].reshape(CELLS, CH))
        xn = (ohat * og[...] + ob[...]).astype(bf16)
        gate = jax.nn.sigmoid(dot(znp, wg[...]))
        up = ct[rows_of(p)].reshape(CELLS, CH).astype(f32) * gate
        gu = up.astype(bf16)
        gxn = dot(gu, wo[...], 1, 1)
        to_channels(tx.at[0, p], norm_back(gxn * og[...], ohat, oinv))
        if p == 0:
            pl.semaphore_wait(barrier, 3 * (DEV - 1))
        launch(0, p)
        update = dot(xn, wo[...])
        gg[here] = (up * update * (1.0 - gate)).astype(bf16)
        add_to(gwo, dot(xn, gu, 0, 0), p == 0)
        add_to(lvec.at[2:3], column_sum(gxn * ohat), p == 0)
        add_to(lvec.at[3:4], column_sum(gxn), p == 0)

    for a, w, wgate, k1, k2 in ((1, wb, wbg, b1, b2), (2, wa, wag, a1, a2)):
        for p in range(NSTEP):
            here = cells(p)
            mask = jnp.broadcast_to(
                rm[rows_of(p)][:, None, :] * km[None], (STEP, BLK, CH)
            ).reshape(CELLS, CH)
            sig = jax.nn.sigmoid(dot(zn[here], wgate[...]))
            masked = mask * sig
            fac = masked * dot(zn[here], w[...])
            to_channels(tx.at[a, p], fac)
            launch(a, p)
            k1[here] = masked
            k2[here] = fac * (1.0 - sig)
    order[...] = turn_order()

    def shuffle(a, p):
        arrive(rbuf.at[a, p], r_recv.at[a, p])
        for t in range(TILES):
            lanes = slice(t * 128, (t + 1) * 128)
            scr[t] = rbuf[a, p, :, :, lanes].reshape(ZN * PROWS, 128).astype(f32)
            for m in range(CPZ):
                sbuf[a, p, m, :, lanes] = scr[t, pl.ds(m, CPROWS, stride=CPZ), :].astype(bf16)

    def divide(p):
        shuffle(0, p)
        keep(sbuf.at[0, p, chip], gq.at[p, odd, chip], g_recv.at[p])

        def send(d):
            t = chip ^ (DEV - d)
            push(
                sbuf.at[0, p, t], gq.at[p, odd, chip], g_send, g_recv.at[p], at_place(2 * t + odd)
            )

        span(DEV, send, 1)

    def exchange(p):
        mine = gq.at[p, odd]
        arrive(mine, g_recv.at[p])
        push(mine, mine, x_send.at[p], x_recv.at[p], {"col": col ^ 1})

    def gather(p):
        arrive(gq.at[p, 1 - odd], x_recv.at[p])
        assemble(lambda y, q: gq[p, q % 2, (y * DEV + q) // 2], asm, gn, p * PN)

    def factor(a, p):
        shuffle(a, p)
        same = odd == a - 1

        def send(d):
            t = chip ^ (DEV - d)
            push(
                sbuf.at[a, p, t],
                fq.at[p, place],
                f_send,
                f_recv.at[p],
                at_place(2 * t + a - 1),
            )

        span(DEV, send, 1)

        @pl.when(same)
        def _():
            keep(sbuf.at[a, p, chip], fq.at[p, place], f_recv.at[p])

        @pl.when(jnp.logical_not(same))
        def _():
            push(
                sbuf.at[a, p, chip], fq.at[p, place], f_send, f_recv.at[p], {"col": col ^ 1}
            )

    divide(0)
    divide(1)
    exchange(0)
    divide(2)
    exchange(1)
    factor(1, 0)
    gather(0)
    exchange(2)
    gather(1)
    factor(1, 1)
    gather(2)

    @pl.when(odd == 0)
    def _():
        left[...] = dot(gn[...], order[...]).astype(bf16)

    @pl.when(odd == 1)
    def _():
        left[...] = dot(order[...], gn[...], 0, 1).astype(bf16)

    factor(1, 2)

    def multiply(p):
        arrive(fq.at[p], f_recv.at[p])
        assemble(lambda y, q: fq[p, y * DEV + q], asm, fn, 0)
        values = dot(left[:, p * PN : (p + 1) * PN], fn[...])
        for t in range(NT):
            add_to(acc.at[t], values[:, t * 128 : (t + 1) * 128], p == 0)

    def give_back():
        for p in range(NSTEP):
            for y in range(2):
                base = p * PN + y * (PN // 2)
                rows = [
                    [acc[t, pl.ds(base + a, CPROWS, stride=PACK), :] for t in range(NT)]
                    for a in range(PACK)
                ]

                def piece(a, q, rows=rows):
                    lo, hi = q * BLK, (q + 1) * BLK
                    first, last = lo // 128, (hi - 1) // 128
                    if first == last:
                        return rows[a][first][:, lo - first * 128 : hi - first * 128]
                    return jnp.concatenate(
                        [
                            rows[a][first][:, lo - first * 128 :],
                            rows[a][last][:, : hi - last * 128],
                        ],
                        axis=1,
                    )

                for q in range(DEV):
                    dis[p, y * DEV + q] = jnp.concatenate(
                        [piece(a, q) for a in range(PACK)], axis=1
                    ).astype(bf16)
            keep(dis.at[p, place], cbuf.at[p, place], c_recv.at[odd, p])

            def send(d, p=p):
                t = place ^ (PLANE - d)
                push(
                    dis.at[p, t], cbuf.at[p, place], c_send, c_recv.at[odd, p], at_place(t)
                )

            span(PLANE, send, 1)

    def relay(h, p):
        arrive(cbuf.at[p, 0 : PLANE // 2], c_recv.at[h, p])
        for t in range(TILES):
            lanes = slice(t * 128, (t + 1) * 128)
            for m in range(CPZ):
                scr[t, pl.ds(m, CPROWS, stride=CPZ), :] = cbuf[p, 2 * m + h, :, lanes].astype(f32)
            hbuf[h, p, :, :, lanes] = scr[t].reshape(ZN, PROWS, 128).astype(bf16)
        scatter_z(lambda t: hbuf.at[h, p, t], rx.at[h, p], h_send, h_recv.at[h, p])

    @pl.when(odd == 0)
    def _():
        multiply(0)
        multiply(1)

    factor(2, 0)

    @pl.when(odd == 0)
    def _():
        multiply(2)
        give_back()

    factor(2, 1)

    @pl.when(odd == 1)
    def _():
        multiply(0)

    relay(0, 0)
    factor(2, 2)

    @pl.when(odd == 1)
    def _():
        multiply(1)

    relay(0, 1)
    relay(0, 2)

    @pl.when(odd == 1)
    def _():
        multiply(2)
        give_back()

    for p in range(NSTEP):
        relay(1, p)

    def grads_of(h, p, k1, k2):
        arrive(rx.at[h, p], h_recv.at[h, p])
        got = from_channels(rx.at[h, p])
        here = cells(p)
        return [(got * k1[here]).astype(bf16), (got * k2[here]).astype(bf16)]

    for p in range(NSTEP):
        here = cells(p)
        grads = jnp.concatenate(grads_of(0, p, a1, a2) + [gg[here]], axis=1)
        gz[here] = dot(grads, wcat[:, : 3 * CH], 1, 1)
        add_to(gwa, dot(zn[here], grads, 0, 0), p == 0)

    for t in range(DEV):
        k, at = divmod(t * EARLY, CH)
        source = gwo[at : at + EARLY, :] if k == 3 else gwa[at : at + EARLY, k * CH : (k + 1) * CH]
        epart[t] = source.astype(bf16)
    scatter("col", lambda t: epart.at[t], eg1, e_send.at[0], e_recv.at[0])

    def last(p):
        here = cells(p)
        grads = jnp.concatenate(grads_of(1, p, b1, b2), axis=1)
        total = gz[here] + dot(grads, wcat[:, 3 * CH :], 1, 1)
        add_to(gwb, dot(zn[here], grads, 0, 0), p == 0)
        add_to(lvec.at[0:1], column_sum(total * hat[here]), p == 0)
        add_to(lvec.at[1:2], column_sum(total), p == 0)
        return total

    def write(p, total):
        here = cells(p)
        value = norm_back(total * lg[...], hat[here], inv[here])
        gp[rows_of(p)] = value.astype(bf16).reshape(STEP, BLK, CH)

    write(0, last(0))
    write(1, last(1))
    total = last(2)

    vector = jnp.concatenate([lvec[...], jnp.zeros((8, CH), f32)], axis=0)
    for t in range(DEV):
        k, at = divmod(t * LATE, CH)
        source = gwb[at : at + LATE, k * CH : (k + 1) * CH]
        lpart[t] = jnp.concatenate([source, vector], axis=0).astype(bf16)
    scatter("col", lambda t: lpart.at[t], lg1, l_send.at[0], l_recv.at[0])
    arrive(eg1, e_recv.at[0])
    emid[...] = jnp.sum(eg1[...].astype(f32), axis=0).astype(bf16)
    scatter("row", lambda t: emid, eg2, e_send.at[1], e_recv.at[1])
    write(2, total)
    arrive(lg1, l_recv.at[0])
    lmid[...] = jnp.sum(lg1[...].astype(f32), axis=0).astype(bf16)
    scatter("row", lambda t: lmid, lg2, l_send.at[1], l_recv.at[1])
    arrive(eg2, e_recv.at[1])
    efin[...] = (jnp.sum(eg2[...].astype(f32), axis=0) * (1.0 / N)).astype(bf16)
    scatter("col", lambda t: efin, eout, e_send.at[2], e_recv.at[2])
    arrive(lg2, l_recv.at[1])
    done = jnp.sum(lg2[...].astype(f32), axis=0) * (1.0 / N)
    vout[...] = done[LATE:]
    lfin[...] = done[:LATE].astype(bf16)
    scatter("col", lambda t: lfin, lout, l_send.at[2], l_recv.at[2])

    for a in range(3):
        arrive(rbuf.at[a, :, 0 : ZN - 1], r_send.at[a])
    arrive(gq.at[:, 0, 0 : DEV - 1], g_send)
    for p in range(NSTEP):
        arrive(gq.at[p, 0], x_send.at[p])
    arrive(fq.at[:, 0 : PLANE - 1], f_send)
    arrive(cbuf.at[:, 0 : PLANE - 1], c_send)
    arrive(hbuf.at[:, :, 0 : ZN - 1], h_send)
    for k in range(3):
        arrive(eg1.at[0 : DEV - 1], e_send.at[k])
    arrive(lg1.at[0 : DEV - 1], l_send.at[0])
    arrive(lg2.at[0 : DEV - 1], l_send.at[1])
    arrive(lout.at[0 : DEV - 1], l_send.at[2])
    arrive(eout, e_recv.at[2])
    arrive(lout, l_recv.at[2])


def whole_step(*args):
    dma = pltpu.SemaphoreType.DMA
    turned = (NSTEP, ZN, PROWS, LANES)
    crossed = (NSTEP, PLANE, CPROWS, LANES)
    flat = (BLK * BLK, CH)
    early = (DEV, EARLY, CH)
    late = (DEV, LATE + 16, CH)

    def wide(*shape):
        return pltpu.VMEM(shape, f32)

    def thin(*shape):
        return pltpu.VMEM(shape, bf16)

    return pl.pallas_call(
        kernel,
        in_specs=[pl.BlockSpec(memory_space=pl.ANY)] * 14,
        out_specs=[VMEM] * 4,
        out_shape=[
            jax.ShapeDtypeStruct((BLK, BLK, CH), bf16),
            jax.ShapeDtypeStruct(early, bf16),
            jax.ShapeDtypeStruct((DEV, LATE, CH), bf16),
            jax.ShapeDtypeStruct((16, CH), f32),
        ],
        scratch_shapes=[
            thin(*flat),
            wide(*flat),
            wide(*flat),
            wide(*flat),
            wide(*flat),
            wide(*flat),
            wide(*flat),
            thin(*flat),
            wide(*flat),
            wide(CH, CH),
            wide(CH, 3 * CH),
            wide(CH, 2 * CH),
            wide(8, CH),
            thin(CH, 5 * CH),
            thin(3, *turned),
            thin(2, *turned),
            thin(3, *turned),
            wide(TILES, ZN * PROWS, 128),
            thin(3, NSTEP, CPZ, CPROWS, LANES),
            thin(NSTEP, 2, DEV, CPROWS, LANES),
            thin(*crossed),
            wide(NT, PN, 128),
            thin(N, N),
            thin(N, N),
            thin(N, N),
            thin(PN, N),
            wide(NT, N, 128),
            thin(*crossed),
            thin(*crossed),
            thin(2, *turned),
            thin(*early),
            thin(*early),
            thin(EARLY, CH),
            thin(*early),
            thin(EARLY, CH),
            thin(*late),
            thin(*late),
            thin(LATE + 16, CH),
            thin(*late),
            thin(LATE, CH),
            dma((3,)),
            dma((3, NSTEP)),
            dma,
            dma((NSTEP,)),
            dma((NSTEP,)),
            dma((NSTEP,)),
            dma,
            dma((NSTEP,)),
            dma,
            dma((2, NSTEP)),
            dma,
            dma((2, NSTEP)),
            dma((3,)),
            dma((3,)),
            dma((3,)),
            dma((3,)),
            dma((14,)),
        ]
        + [pltpu.VMEM(a.shape, a.dtype) for a in args],
        name="whole_step",
        compiler_params=pltpu.CompilerParams(
            collective_id=1, has_side_effects=True, vmem_limit_bytes=LIMIT
        ),
    )(*args)


def finish_kernel(pair, early, late, vec, *outs):
    outs[0][...] = pair[...]
    place = (1, 2, 5, 6)
    for t in range(DEV):
        k, at = divmod(t * EARLY, CH)
        outs[place[k]][at : at + EARLY, :] = early[t].astype(f32)
        k, at = divmod(t * LATE, CH)
        outs[3 + k][at : at + LATE, :] = late[t].astype(f32)
    for k in range(4):
        outs[7 + k][...] = vec[k : k + 1]


def finish(*args):
    return pl.pallas_call(
        finish_kernel,
        in_specs=[VMEM] * 4,
        out_specs=[VMEM] * 11,
        out_shape=[jax.ShapeDtypeStruct((BLK, BLK, CH), bf16)]
        + [jax.ShapeDtypeStruct((CH, CH), f32)] * 6
        + [jax.ShapeDtypeStruct((1, CH), f32)] * 4,
        name="finish",
    )(*args)


def body(
    pair_map,
    saved_product,
    cotangent,
    residue_mask,
    ln_gain,
    ln_bias,
    out_gain,
    out_bias,
    *weights,
):
    vecs = [v.reshape(1, CH) for v in (ln_gain, ln_bias, out_gain, out_bias)]
    outs = finish(
        *whole_step(
            pair_map, saved_product, cotangent, residue_mask.reshape(NT, CH), *vecs, *weights
        )
    )
    return tuple(outs[:7]) + tuple(v.reshape(CH) for v in outs[7:])


def solution(mesh):
    return jax.shard_map(
        body,
        mesh=mesh,
        in_specs=(P("row", "col", None),) * 3 + (P(),) * 11,
        out_specs=(P("row", "col", None),) + (P(),) * 10,
        check_vma=False,
    )
```

```python
import jax
import jax.numpy as jnp
from jax import lax
from jax.experimental import pallas as pl
from jax.experimental.pallas import tpu as pltpu
from jax.sharding import PartitionSpec as P

MESH = pl.DeviceIdType.MESH
f32 = jnp.float32
bf16 = jnp.bfloat16
epsilon = 1e-05
VMEM = pl.BlockSpec(memory_space=pltpu.VMEM)
LIMIT = 56 << 20

DEV = 16
BLK = 48
CH = 128
PACK = 8
LANES = PACK * BLK
TILES = LANES // 128
ZN = 8
HALF = DEV // 2
CPZ = CH // ZN
N = DEV * BLK
STEP = 16
CELLS = STEP * BLK
NSTEP = BLK // STEP
EARLY = 4 * CH // DEV
LATE = 2 * CH // DEV
PROWS = STEP // PACK * CPZ
CPROWS = STEP // PACK * ZN
PN = STEP * DEV
NT = N // 128


def dot(a, b, ca=1, cb=0):
    return lax.dot_general(a, b, (((ca,), (cb,)), ((), ())), preferred_element_type=f32)


def mean(v):
    return jnp.mean(v, axis=-1, keepdims=True)


def normalize(values):
    values = values.astype(f32)
    centred = values - mean(values)
    inverse = lax.rsqrt(mean(centred * centred) + epsilon)
    return centred * inverse, inverse


def norm_back(scaled, normed, inverse):
    return inverse * (scaled - mean(scaled) - normed * mean(scaled * normed))


def to_channels(ref, values):
    halves = []
    for g in range(STEP // PACK):
        turned = values[g * LANES : (g + 1) * LANES].T
        halves.append(turned.reshape(ZN, CPZ, LANES))
    ref[...] = jnp.concatenate(halves, axis=1).astype(bf16)


def from_channels(ref):
    values = ref[...].astype(f32)
    parts = []
    for g in range(STEP // PACK):
        parts.append(values[:, g * CPZ : (g + 1) * CPZ, :].reshape(CH, LANES).T)
    return jnp.concatenate(parts, axis=0)


def add_to(ref, values, first):
    if first:
        ref[...] = values
    else:
        ref[...] += values


def column_sum(values):
    return jnp.sum(values, axis=0, keepdims=True)


def mask_of(rmask, axis):
    first = lax.axis_index(axis) * BLK
    lane = lax.broadcasted_iota(jnp.int32, (BLK, CH), 1)
    sub = lax.broadcasted_iota(jnp.int32, (BLK, CH), 0)
    picked = jnp.zeros((BLK, CH), f32)
    for t in range(NT):
        here = lane + t * CH == sub + first
        picked += jnp.where(here, rmask[t : t + 1, :].astype(f32), 0.0)
    return jnp.broadcast_to(jnp.sum(picked, axis=1, keepdims=True), (BLK, CH))


def peer(axis, d):
    return lax.axis_index(axis) ^ d


def span(count, action, start=0):
    def run(d, carry):
        action(d)
        return carry

    lax.fori_loop(start, count, run, 0)


def arrive(ref, sem):
    pltpu.make_async_copy(ref, ref, sem).wait()


def push(src, dst, send, recv, where):
    pltpu.make_async_remote_copy(
        src_ref=src,
        dst_ref=dst,
        send_sem=send,
        recv_sem=recv,
        device_id=where,
        device_id_type=MESH,
    ).start()


def keep(src, dst, sem):
    pltpu.make_async_copy(src, dst, sem).start()


def scatter_z(src, dst, send, recv):
    row = lax.axis_index("row")
    z = row >> 1
    keep(src(z), dst.at[z], recv)

    def go(d):
        k = ZN - d
        away = jnp.where((k & 1) == 1, (k + 1) >> 1, ZN - (k >> 1))
        t = (z + away) & (ZN - 1)
        push(src(t), dst.at[z], send, recv, {"row": 2 * t + (row & 1)})

    span(ZN, go, 1)


def scatter(axis, src, dst, send, recv):
    me = lax.axis_index(axis)
    keep(src(me), dst.at[me], recv)

    def go(d):
        t = peer(axis, DEV - d)
        push(src(t), dst.at[me], send, recv, {axis: t})

    span(DEV, go, 1)


def assemble(pick, count, scr, dst, first):
    tiles = count * BLK // 128
    for y in range(2):
        for a in range(PACK):
            rows = jnp.concatenate(
                [pick(y, q)[:, a * BLK : (a + 1) * BLK].astype(f32) for q in range(count)], axis=1
            )
            for t in range(tiles):
                scr[t, pl.ds(y * (PN // 2) + a, CPROWS, stride=PACK), :] = rows[
                    :, t * 128 : (t + 1) * 128
                ]
    for t in range(tiles):
        dst[first : first + PN, t * 128 : (t + 1) * 128] = scr[t].astype(bf16)


def turn_order():
    lane = lax.broadcasted_iota(jnp.int32, (N, N), 1)
    sub = lax.broadcasted_iota(jnp.int32, (N, N), 0)
    piece = lane >> 8
    device = 2 * ((lane >> 4) & 7) + ((lane >> 7) & 1)
    place = device * BLK + piece * STEP + (lane & 15)
    return jnp.where(place == sub, 1.0, 0.0).astype(bf16)


def kernel(
    *refs
):
    given, refs = refs[:14], refs[14:]
    (
        gp, eout, lout, vout,
        zn, hat, inv, a1, a2, b1, b2, gg, gz, gwo, gwa, gwb, lvec, wcat, tx, rx,
        rbuf, scr, sbuf, gq, fq, asm, gn, left, below, order, fn, acc, dis, cbuf, hbuf,
        epart, eg1, emid, eg2, efin, lpart, lg1, lmid, lg2, lfin,
        r_send, r_recv, g_send, g_recv, x_send, x_recv, f_send, f_recv,
        c_send, c_recv, h_send, h_recv, e_send, e_recv, l_send, l_recv, i_recv,
        *held
    ) = refs
    (
        pm, sp, ct, rmask, lg, lb, og, ob, wa, wag, wb, wbg, wg, wo,
    ) = held
    row, col = lax.axis_index("row"), lax.axis_index("col")
    odd = col & 1
    place = (row & 1) * DEV + col
    chip = place >> 1

    def at_place(t):
        return {"row": row - (row & 1) + (t >> 4), "col": t & (DEV - 1)}

    barrier = pltpu.get_barrier_semaphore()
    for axis in ("row", "col"):

        def hello(d, axis=axis):
            pl.semaphore_signal(
                barrier, inc=1, device_id={axis: peer(axis, d)}, device_id_type=MESH
            )

        span(DEV, hello, 1)

    def hello_plane(d):
        pl.semaphore_signal(
            barrier, inc=1, device_id={"row": row ^ 1, "col": col ^ d}, device_id_type=MESH
        )

    span(DEV, hello_plane, 1)

    for k in range(14):
        keep(given[k], held[k], i_recv.at[k])
    lvec[...] = jnp.zeros((8, CH), f32)
    for k in range(14):
        arrive(held[k], i_recv.at[k])
    rm = mask_of(rmask, "row")
    km = mask_of(rmask, "col")
    for k, w in enumerate((wa, wag, wg, wb, wbg)):
        wcat[:, k * CH : (k + 1) * CH] = w[...]

    def cells(p):
        return slice(p * CELLS, (p + 1) * CELLS)

    def rows_of(p):
        return slice(p * STEP, (p + 1) * STEP)

    def launch(a, p):
        scatter_z(lambda t: tx.at[a, p, t], rbuf.at[a, p], r_send.at[a], r_recv.at[a, p])

    for p in range(NSTEP):
        here = cells(p)
        phat, pinv = normalize(pm[rows_of(p)].reshape(CELLS, CH))
        hat[here] = phat
        inv[here] = jnp.broadcast_to(pinv, (CELLS, CH))
        znp = (phat * lg[...] + lb[...]).astype(bf16)
        zn[here] = znp
        ohat, oinv = normalize(sp[rows_of(p)].reshape(CELLS, CH))
        xn = (ohat * og[...] + ob[...]).astype(bf16)
        gate = jax.nn.sigmoid(dot(znp, wg[...]))
        up = ct[rows_of(p)].reshape(CELLS, CH).astype(f32) * gate
        gu = up.astype(bf16)
        gxn = dot(gu, wo[...], 1, 1)
        to_channels(tx.at[0, p], norm_back(gxn * og[...], ohat, oinv))
        if p == 0:
            pl.semaphore_wait(barrier, 3 * (DEV - 1))
        launch(0, p)
        update = dot(xn, wo[...])
        gg[here] = (up * update * (1.0 - gate)).astype(bf16)
        add_to(gwo, dot(xn, gu, 0, 0), p == 0)
        add_to(lvec.at[2:3], column_sum(gxn * ohat), p == 0)
        add_to(lvec.at[3:4], column_sum(gxn), p == 0)

    for a, w, wgate, k1, k2 in ((1, wb, wbg, b1, b2), (2, wa, wag, a1, a2)):
        for p in range(NSTEP):
            here = cells(p)
            mask = jnp.broadcast_to(
                rm[rows_of(p)][:, None, :] * km[None], (STEP, BLK, CH)
            ).reshape(CELLS, CH)
            sig = jax.nn.sigmoid(dot(zn[here], wgate[...]))
            masked = mask * sig
            fac = masked * dot(zn[here], w[...])
            to_channels(tx.at[a, p], fac)
            launch(a, p)
            k1[here] = masked
            k2[here] = fac * (1.0 - sig)
    order[...] = turn_order()

    def shuffle(a, p):
        arrive(rbuf.at[a, p], r_recv.at[a, p])
        for t in range(TILES):
            lanes = slice(t * 128, (t + 1) * 128)
            scr[t] = rbuf[a, p, :, :, lanes].reshape(ZN * PROWS, 128).astype(f32)
            for m in range(CPZ):
                sbuf[a, p, m, :, lanes] = scr[t, pl.ds(m, CPROWS, stride=CPZ), :].astype(bf16)

    def divide(p):
        shuffle(0, p)
        keep(sbuf.at[0, p, chip], gq.at[p, odd, chip], g_recv.at[p])

        def send(d):
            t = chip ^ (DEV - d)
            push(
                sbuf.at[0, p, t], gq.at[p, odd, chip], g_send, g_recv.at[p], at_place(2 * t + odd)
            )

        span(DEV, send, 1)

    def exchange(p):
        mine = gq.at[p, odd]
        arrive(mine, g_recv.at[p])
        push(mine, mine, x_send.at[p], x_recv.at[p], {"col": col ^ 1})

    def gather(p):
        arrive(gq.at[p, 1 - odd], x_recv.at[p])
        assemble(lambda y, q: gq[p, q % 2, (y * DEV + q) // 2], DEV, asm, gn, p * PN)

    def factor(a, p):
        shuffle(a, p)
        h = a - 1
        keep(sbuf.at[a, p, chip], fq.at[h, p, chip], f_recv.at[h, p])

        def send(d):
            t = chip ^ (DEV - d)
            push(
                sbuf.at[a, p, t], fq.at[h, p, chip], f_send, f_recv.at[h, p], at_place(2 * t + odd)
            )

        span(DEV, send, 1)

    divide(0)
    divide(1)
    exchange(0)
    divide(2)
    exchange(1)
    factor(1, 0)
    gather(0)
    exchange(2)
    gather(1)
    factor(1, 1)
    gather(2)

    left[...] = dot(gn[...], order[...]).astype(bf16)
    factor(1, 2)

    def multiply(h, p):
        arrive(fq.at[h, p], f_recv.at[h, p])
        assemble(lambda y, j: fq[h, p, y * HALF + j], HALF, asm, fn, 0)
        sides = (left, below)[h]
        values = dot(sides[:, p * PN : (p + 1) * PN], fn[...])
        for t in range(NT // 2):
            add_to(acc.at[t], values[:, t * 128 : (t + 1) * 128], p == 0)

    def give_back(h):
        for p in range(NSTEP):
            for y in range(2):
                base = p * PN + y * (PN // 2)
                rows = [
                    [acc[t, pl.ds(base + a, CPROWS, stride=PACK), :] for t in range(NT // 2)]
                    for a in range(PACK)
                ]

                def piece(a, j, rows=rows):
                    lo, hi = j * BLK, (j + 1) * BLK
                    first, last = lo // 128, (hi - 1) // 128
                    if first == last:
                        return rows[a][first][:, lo - first * 128 : hi - first * 128]
                    return jnp.concatenate(
                        [
                            rows[a][first][:, lo - first * 128 :],
                            rows[a][last][:, : hi - last * 128],
                        ],
                        axis=1,
                    )

                for j in range(HALF):
                    dis[h, p, y * HALF + j] = jnp.concatenate(
                        [piece(a, j) for a in range(PACK)], axis=1
                    ).astype(bf16)
            keep(dis.at[h, p, chip], cbuf.at[h, p, chip], c_recv.at[h, p])

            def send(d, p=p):
                t = chip ^ (DEV - d)
                push(
                    dis.at[h, p, t],
                    cbuf.at[h, p, chip],
                    c_send,
                    c_recv.at[h, p],
                    at_place(2 * t + odd),
                )

            span(DEV, send, 1)

    def relay(h, p):
        arrive(cbuf.at[h, p], c_recv.at[h, p])
        for t in range(TILES):
            lanes = slice(t * 128, (t + 1) * 128)
            for m in range(CPZ):
                scr[t, pl.ds(m, CPROWS, stride=CPZ), :] = cbuf[h, p, m, :, lanes].astype(f32)
            hbuf[h, p, :, :, lanes] = scr[t].reshape(ZN, PROWS, 128).astype(bf16)
        scatter_z(lambda t: hbuf.at[h, p, t], rx.at[h, p], h_send, h_recv.at[h, p])

    multiply(0, 0)
    multiply(0, 1)
    multiply(0, 2)
    give_back(0)
    factor(2, 0)
    below[...] = dot(order[...], gn[...], 0, 1).astype(bf16)
    factor(2, 1)
    relay(0, 0)
    multiply(1, 0)
    factor(2, 2)
    relay(0, 1)
    multiply(1, 1)
    relay(0, 2)
    multiply(1, 2)
    give_back(1)

    for p in range(NSTEP):
        relay(1, p)

    def grads_of(h, p, k1, k2):
        arrive(rx.at[h, p], h_recv.at[h, p])
        got = from_channels(rx.at[h, p])
        here = cells(p)
        return [(got * k1[here]).astype(bf16), (got * k2[here]).astype(bf16)]

    for p in range(NSTEP):
        here = cells(p)
        grads = jnp.concatenate(grads_of(0, p, a1, a2) + [gg[here]], axis=1)
        gz[here] = dot(grads, wcat[:, : 3 * CH], 1, 1)
        add_to(gwa, dot(zn[here], grads, 0, 0), p == 0)

    for t in range(DEV):
        k, at = divmod(t * EARLY, CH)
        source = gwo[at : at + EARLY, :] if k == 3 else gwa[at : at + EARLY, k * CH : (k + 1) * CH]
        epart[t] = source.astype(bf16)
    scatter("col", lambda t: epart.at[t], eg1, e_send.at[0], e_recv.at[0])

    def last(p):
        here = cells(p)
        grads = jnp.concatenate(grads_of(1, p, b1, b2), axis=1)
        total = gz[here] + dot(grads, wcat[:, 3 * CH :], 1, 1)
        add_to(gwb, dot(zn[here], grads, 0, 0), p == 0)
        add_to(lvec.at[0:1], column_sum(total * hat[here]), p == 0)
        add_to(lvec.at[1:2], column_sum(total), p == 0)
        return total

    def write(p, total):
        here = cells(p)
        value = norm_back(total * lg[...], hat[here], inv[here])
        gp[rows_of(p)] = value.astype(bf16).reshape(STEP, BLK, CH)

    write(0, last(0))
    write(1, last(1))
    total = last(2)

    vector = jnp.concatenate([lvec[...], jnp.zeros((8, CH), f32)], axis=0)
    for t in range(DEV):
        k, at = divmod(t * LATE, CH)
        source = gwb[at : at + LATE, k * CH : (k + 1) * CH]
        lpart[t] = jnp.concatenate([source, vector], axis=0).astype(bf16)
    scatter("col", lambda t: lpart.at[t], lg1, l_send.at[0], l_recv.at[0])
    arrive(eg1, e_recv.at[0])
    emid[...] = jnp.sum(eg1[...].astype(f32), axis=0).astype(bf16)
    scatter("row", lambda t: emid, eg2, e_send.at[1], e_recv.at[1])
    write(2, total)
    arrive(lg1, l_recv.at[0])
    lmid[...] = jnp.sum(lg1[...].astype(f32), axis=0).astype(bf16)
    scatter("row", lambda t: lmid, lg2, l_send.at[1], l_recv.at[1])
    arrive(eg2, e_recv.at[1])
    efin[...] = (jnp.sum(eg2[...].astype(f32), axis=0) * (1.0 / N)).astype(bf16)
    scatter("col", lambda t: efin, eout, e_send.at[2], e_recv.at[2])
    arrive(lg2, l_recv.at[1])
    done = jnp.sum(lg2[...].astype(f32), axis=0) * (1.0 / N)
    vout[...] = done[LATE:]
    lfin[...] = done[:LATE].astype(bf16)
    scatter("col", lambda t: lfin, lout, l_send.at[2], l_recv.at[2])

    for a in range(3):
        arrive(rbuf.at[a, :, 0 : ZN - 1], r_send.at[a])
    arrive(gq.at[:, 0, 0 : DEV - 1], g_send)
    for p in range(NSTEP):
        arrive(gq.at[p, 0], x_send.at[p])
    arrive(fq.at[:, :, 0 : DEV - 1], f_send)
    arrive(cbuf.at[:, :, 0 : DEV - 1], c_send)
    arrive(hbuf.at[:, :, 0 : ZN - 1], h_send)
    for k in range(3):
        arrive(eg1.at[0 : DEV - 1], e_send.at[k])
    arrive(lg1.at[0 : DEV - 1], l_send.at[0])
    arrive(lg2.at[0 : DEV - 1], l_send.at[1])
    arrive(lout.at[0 : DEV - 1], l_send.at[2])
    arrive(eout, e_recv.at[2])
    arrive(lout, l_recv.at[2])


def whole_step(*args):
    dma = pltpu.SemaphoreType.DMA
    turned = (NSTEP, ZN, PROWS, LANES)
    crossed = (2, NSTEP, DEV, CPROWS, LANES)
    flat = (BLK * BLK, CH)
    early = (DEV, EARLY, CH)
    late = (DEV, LATE + 16, CH)

    def wide(*shape):
        return pltpu.VMEM(shape, f32)

    def thin(*shape):
        return pltpu.VMEM(shape, bf16)

    return pl.pallas_call(
        kernel,
        in_specs=[pl.BlockSpec(memory_space=pl.ANY)] * 14,
        out_specs=[VMEM] * 4,
        out_shape=[
            jax.ShapeDtypeStruct((BLK, BLK, CH), bf16),
            jax.ShapeDtypeStruct(early, bf16),
            jax.ShapeDtypeStruct((DEV, LATE, CH), bf16),
            jax.ShapeDtypeStruct((16, CH), f32),
        ],
        scratch_shapes=[
            thin(*flat),
            wide(*flat),
            wide(*flat),
            wide(*flat),
            wide(*flat),
            wide(*flat),
            wide(*flat),
            thin(*flat),
            wide(*flat),
            wide(CH, CH),
            wide(CH, 3 * CH),
            wide(CH, 2 * CH),
            wide(8, CH),
            thin(CH, 5 * CH),
            thin(3, *turned),
            thin(2, *turned),
            thin(3, *turned),
            wide(TILES, ZN * PROWS, 128),
            thin(3, NSTEP, CPZ, CPROWS, LANES),
            thin(NSTEP, 2, DEV, CPROWS, LANES),
            thin(*crossed),
            wide(NT, PN, 128),
            thin(N, N),
            thin(N, N),
            thin(N, N),
            thin(N, N),
            thin(PN, N // 2),
            wide(NT // 2, N, 128),
            thin(*crossed),
            thin(*crossed),
            thin(2, *turned),
            thin(*early),
            thin(*early),
            thin(EARLY, CH),
            thin(*early),
            thin(EARLY, CH),
            thin(*late),
            thin(*late),
            thin(LATE + 16, CH),
            thin(*late),
            thin(LATE, CH),
            dma((3,)),
            dma((3, NSTEP)),
            dma,
            dma((NSTEP,)),
            dma((NSTEP,)),
            dma((NSTEP,)),
            dma,
            dma((2, NSTEP)),
            dma,
            dma((2, NSTEP)),
            dma,
            dma((2, NSTEP)),
            dma((3,)),
            dma((3,)),
            dma((3,)),
            dma((3,)),
            dma((14,)),
        ]
        + [pltpu.VMEM(a.shape, a.dtype) for a in args],
        name="whole_step",
        compiler_params=pltpu.CompilerParams(
            collective_id=1, has_side_effects=True, vmem_limit_bytes=LIMIT
        ),
    )(*args)


def finish_kernel(pair, early, late, vec, *outs):
    outs[0][...] = pair[...]
    place = (1, 2, 5, 6)
    for t in range(DEV):
        k, at = divmod(t * EARLY, CH)
        outs[place[k]][at : at + EARLY, :] = early[t].astype(f32)
        k, at = divmod(t * LATE, CH)
        outs[3 + k][at : at + LATE, :] = late[t].astype(f32)
    for k in range(4):
        outs[7 + k][...] = vec[k : k + 1]


def finish(*args):
    return pl.pallas_call(
        finish_kernel,
        in_specs=[VMEM] * 4,
        out_specs=[VMEM] * 11,
        out_shape=[jax.ShapeDtypeStruct((BLK, BLK, CH), bf16)]
        + [jax.ShapeDtypeStruct((CH, CH), f32)] * 6
        + [jax.ShapeDtypeStruct((1, CH), f32)] * 4,
        name="finish",
    )(*args)


def body(
    pair_map,
    saved_product,
    cotangent,
    residue_mask,
    ln_gain,
    ln_bias,
    out_gain,
    out_bias,
    *weights,
):
    vecs = [v.reshape(1, CH) for v in (ln_gain, ln_bias, out_gain, out_bias)]
    outs = finish(
        *whole_step(
            pair_map, saved_product, cotangent, residue_mask.reshape(NT, CH), *vecs, *weights
        )
    )
    return tuple(outs[:7]) + tuple(v.reshape(CH) for v in outs[7:])


def solution(mesh):
    return jax.shard_map(
        body,
        mesh=mesh,
        in_specs=(P("row", "col", None),) * 3 + (P(),) * 11,
        out_specs=(P("row", "col", None),) + (P(),) * 10,
        check_vma=False,
    )
```

```python
import jax
import jax.numpy as jnp
from jax import lax
from jax.experimental import pallas as pl
from jax.experimental.pallas import tpu as pltpu
from jax.sharding import PartitionSpec as P

MESH = pl.DeviceIdType.MESH
f32 = jnp.float32
bf16 = jnp.bfloat16
epsilon = 1e-05
VMEM = pl.BlockSpec(memory_space=pltpu.VMEM)
LIMIT = 56 << 20

DEV = 16
BLK = 48
CH = 128
PACK = 8
LANES = PACK * BLK
TILES = LANES // 128
ZN = 8
HALF = DEV // 2
CPZ = CH // ZN
N = DEV * BLK
STEP = 16
CELLS = STEP * BLK
NSTEP = BLK // STEP
EARLY = 4 * CH // DEV
LATE = 2 * CH // DEV
PROWS = STEP // PACK * CPZ
CPROWS = STEP // PACK * ZN
PN = STEP * DEV
NT = N // 128


def dot(a, b, ca=1, cb=0):
    return lax.dot_general(a, b, (((ca,), (cb,)), ((), ())), preferred_element_type=f32)


def mean(v):
    return jnp.mean(v, axis=-1, keepdims=True)


def normalize(values):
    values = values.astype(f32)
    centred = values - mean(values)
    inverse = lax.rsqrt(mean(centred * centred) + epsilon)
    return centred * inverse, inverse


def norm_back(scaled, normed, inverse):
    return inverse * (scaled - mean(scaled) - normed * mean(scaled * normed))


def to_channels(ref, values):
    halves = []
    for g in range(STEP // PACK):
        turned = values[g * LANES : (g + 1) * LANES].T
        halves.append(turned.reshape(ZN, CPZ, LANES))
    ref[...] = jnp.concatenate(halves, axis=1).astype(bf16)


def from_channels(ref):
    values = ref[...].astype(f32)
    parts = []
    for g in range(STEP // PACK):
        parts.append(values[:, g * CPZ : (g + 1) * CPZ, :].reshape(CH, LANES).T)
    return jnp.concatenate(parts, axis=0)


def add_to(ref, values, first):
    if first:
        ref[...] = values
    else:
        ref[...] += values


def column_sum(values):
    return jnp.sum(values, axis=0, keepdims=True)


def mask_of(rmask, axis):
    first = lax.axis_index(axis) * BLK
    lane = lax.broadcasted_iota(jnp.int32, (BLK, CH), 1)
    sub = lax.broadcasted_iota(jnp.int32, (BLK, CH), 0)
    picked = jnp.zeros((BLK, CH), f32)
    for t in range(NT):
        here = lane + t * CH == sub + first
        picked += jnp.where(here, rmask[t : t + 1, :].astype(f32), 0.0)
    return jnp.broadcast_to(jnp.sum(picked, axis=1, keepdims=True), (BLK, CH))


def peer(axis, d):
    return lax.axis_index(axis) ^ d


def span(count, action, start=0):
    def run(d, carry):
        action(d)
        return carry

    lax.fori_loop(start, count, run, 0)


def arrive(ref, sem):
    pltpu.make_async_copy(ref, ref, sem).wait()


def push(src, dst, send, recv, where):
    pltpu.make_async_remote_copy(
        src_ref=src,
        dst_ref=dst,
        send_sem=send,
        recv_sem=recv,
        device_id=where,
        device_id_type=MESH,
    ).start()


def keep(src, dst, sem):
    pltpu.make_async_copy(src, dst, sem).start()


def scatter_z(src, dst, send, recv):
    row = lax.axis_index("row")
    z = row >> 1
    keep(src(z), dst.at[z], recv)

    def go(d):
        k = ZN - d
        away = jnp.where((k & 1) == 1, (k + 1) >> 1, ZN - (k >> 1))
        t = (z + away) & (ZN - 1)
        push(src(t), dst.at[z], send, recv, {"row": 2 * t + (row & 1)})

    span(ZN, go, 1)


def scatter(axis, src, dst, send, recv):
    me = lax.axis_index(axis)
    keep(src(me), dst.at[me], recv)

    def go(d):
        t = peer(axis, DEV - d)
        push(src(t), dst.at[me], send, recv, {axis: t})

    span(DEV, go, 1)


def assemble(pick, count, scr, dst, first):
    tiles = count * BLK // 128
    for y in range(2):
        for a in range(PACK):
            rows = jnp.concatenate(
                [pick(y, q)[:, a * BLK : (a + 1) * BLK].astype(f32) for q in range(count)], axis=1
            )
            for t in range(tiles):
                scr[t, pl.ds(y * (PN // 2) + a, CPROWS, stride=PACK), :] = rows[
                    :, t * 128 : (t + 1) * 128
                ]
    for t in range(tiles):
        dst[first : first + PN, t * 128 : (t + 1) * 128] = scr[t].astype(bf16)


def turn_order():
    lane = lax.broadcasted_iota(jnp.int32, (N, N), 1)
    sub = lax.broadcasted_iota(jnp.int32, (N, N), 0)
    piece = lane >> 8
    device = 2 * ((lane >> 4) & 7) + ((lane >> 7) & 1)
    place = device * BLK + piece * STEP + (lane & 15)
    return jnp.where(place == sub, 1.0, 0.0).astype(bf16)


def kernel(
    *refs
):
    given, refs = refs[:14], refs[14:]
    (
        gp, eout, lout, vout,
        zn, hat, inv, a1, a2, b1, b2, gg, gz, gwo, gwa, gwb, lvec, wcat, tx, rx,
        rbuf, scr, sbuf, gq, fq, asm, gn, left, below, order, fn, acc, dis, cbuf, hbuf,
        epart, eg1, emid, eg2, efin, lpart, lg1, lmid, lg2, lfin,
        r_send, r_recv, g_send, g_recv, x_send, x_recv, f_send, f_recv,
        c_send, c_recv, h_send, h_recv, e_send, e_recv, l_send, l_recv, i_recv,
        *held
    ) = refs
    (
        pm, sp, ct, rmask, lg, lb, og, ob, wa, wag, wb, wbg, wg, wo,
    ) = held
    row, col = lax.axis_index("row"), lax.axis_index("col")
    odd = col & 1
    place = (row & 1) * DEV + col
    chip = place >> 1

    def at_place(t):
        return {"row": row - (row & 1) + (t >> 4), "col": t & (DEV - 1)}

    barrier = pltpu.get_barrier_semaphore()
    for axis in ("row", "col"):

        def hello(d, axis=axis):
            pl.semaphore_signal(
                barrier, inc=1, device_id={axis: peer(axis, d)}, device_id_type=MESH
            )

        span(DEV, hello, 1)

    def hello_plane(d):
        pl.semaphore_signal(
            barrier, inc=1, device_id={"row": row ^ 1, "col": col ^ d}, device_id_type=MESH
        )

    span(DEV, hello_plane, 1)

    for k in range(14):
        keep(given[k], held[k], i_recv.at[k])
    lvec[...] = jnp.zeros((8, CH), f32)
    for k in range(14):
        arrive(held[k], i_recv.at[k])
    rm = mask_of(rmask, "row")
    km = mask_of(rmask, "col")
    for k, w in enumerate((wa, wag, wg, wb, wbg)):
        wcat[:, k * CH : (k + 1) * CH] = w[...]

    def cells(p):
        return slice(p * CELLS, (p + 1) * CELLS)

    def rows_of(p):
        return slice(p * STEP, (p + 1) * STEP)

    def launch(a, p):
        scatter_z(lambda t: tx.at[a, p, t], rbuf.at[a, p], r_send.at[a], r_recv.at[a, p])

    for p in range(NSTEP):
        here = cells(p)
        phat, pinv = normalize(pm[rows_of(p)].reshape(CELLS, CH))
        hat[here] = phat
        inv[here] = jnp.broadcast_to(pinv, (CELLS, CH))
        znp = (phat * lg[...] + lb[...]).astype(bf16)
        zn[here] = znp
        ohat, oinv = normalize(sp[rows_of(p)].reshape(CELLS, CH))
        xn = (ohat * og[...] + ob[...]).astype(bf16)
        gate = jax.nn.sigmoid(dot(znp, wg[...]))
        up = ct[rows_of(p)].reshape(CELLS, CH).astype(f32) * gate
        gu = up.astype(bf16)
        gxn = dot(gu, wo[...], 1, 1)
        to_channels(tx.at[0, p], norm_back(gxn * og[...], ohat, oinv))
        if p == 0:
            pl.semaphore_wait(barrier, 3 * (DEV - 1))
        launch(0, p)
        update = dot(xn, wo[...])
        gg[here] = (up * update * (1.0 - gate)).astype(bf16)
        add_to(gwo, dot(xn, gu, 0, 0), p == 0)
        add_to(lvec.at[2:3], column_sum(gxn * ohat), p == 0)
        add_to(lvec.at[3:4], column_sum(gxn), p == 0)

    for a, w, wgate, k1, k2 in ((1, wb, wbg, b1, b2), (2, wa, wag, a1, a2)):
        for p in range(NSTEP):
            here = cells(p)
            mask = jnp.broadcast_to(
                rm[rows_of(p)][:, None, :] * km[None], (STEP, BLK, CH)
            ).reshape(CELLS, CH)
            sig = jax.nn.sigmoid(dot(zn[here], wgate[...]))
            masked = mask * sig
            fac = masked * dot(zn[here], w[...])
            to_channels(tx.at[a, p], fac)
            launch(a, p)
            k1[here] = masked
            k2[here] = fac * (1.0 - sig)
    order[...] = turn_order()

    def shuffle(a, p):
        arrive(rbuf.at[a, p], r_recv.at[a, p])
        for t in range(TILES):
            lanes = slice(t * 128, (t + 1) * 128)
            scr[t] = rbuf[a, p, :, :, lanes].reshape(ZN * PROWS, 128).astype(f32)
            for m in range(CPZ):
                sbuf[a, p, m, :, lanes] = scr[t, pl.ds(m, CPROWS, stride=CPZ), :].astype(bf16)

    def divide(p):
        shuffle(0, p)
        keep(sbuf.at[0, p, chip], gq.at[p, odd, chip], g_recv.at[p])

        def send(d):
            t = chip ^ (DEV - d)
            push(
                sbuf.at[0, p, t], gq.at[p, odd, chip], g_send, g_recv.at[p], at_place(2 * t + odd)
            )

        span(DEV, send, 1)

    def exchange(p):
        mine = gq.at[p, odd]
        arrive(mine, g_recv.at[p])
        push(mine, mine, x_send.at[p], x_recv.at[p], {"col": col ^ 1})

    def gather(p):
        arrive(gq.at[p, 1 - odd], x_recv.at[p])
        assemble(lambda y, q: gq[p, q % 2, (y * DEV + q) // 2], DEV, asm, gn, p * PN)

    def factor(a, p):
        shuffle(a, p)
        h = a - 1
        keep(sbuf.at[a, p, chip], fq.at[h, p, chip], f_recv.at[h, p])

        def send(d):
            t = chip ^ (DEV - d)
            push(
                sbuf.at[a, p, t], fq.at[h, p, chip], f_send, f_recv.at[h, p], at_place(2 * t + odd)
            )

        span(DEV, send, 1)

    divide(0)
    divide(1)
    exchange(0)
    divide(2)
    exchange(1)
    factor(1, 0)
    gather(0)
    exchange(2)
    gather(1)
    factor(1, 1)
    gather(2)

    left[...] = dot(gn[...], order[...]).astype(bf16)
    factor(1, 2)

    def multiply(h, p):
        arrive(fq.at[h, p], f_recv.at[h, p])
        assemble(lambda y, j: fq[h, p, y * HALF + j], HALF, asm, fn, 0)
        sides = (left, below)[h]
        values = dot(sides[:, p * PN : (p + 1) * PN], fn[...])
        for t in range(NT // 2):
            add_to(acc.at[t], values[:, t * 128 : (t + 1) * 128], p == 0)

    def give_back(h):
        for p in range(NSTEP):
            for y in range(2):
                base = p * PN + y * (PN // 2)
                rows = [
                    [acc[t, pl.ds(base + a, CPROWS, stride=PACK), :] for t in range(NT // 2)]
                    for a in range(PACK)
                ]

                def piece(a, j, rows=rows):
                    lo, hi = j * BLK, (j + 1) * BLK
                    first, last = lo // 128, (hi - 1) // 128
                    if first == last:
                        return rows[a][first][:, lo - first * 128 : hi - first * 128]
                    return jnp.concatenate(
                        [
                            rows[a][first][:, lo - first * 128 :],
                            rows[a][last][:, : hi - last * 128],
                        ],
                        axis=1,
                    )

                for j in range(HALF):
                    dis[h, p, y * HALF + j] = jnp.concatenate(
                        [piece(a, j) for a in range(PACK)], axis=1
                    ).astype(bf16)
            keep(dis.at[h, p, chip], cbuf.at[h, p, chip], c_recv.at[h, p])

            def send(d, p=p):
                t = chip ^ (DEV - d)
                push(
                    dis.at[h, p, t],
                    cbuf.at[h, p, chip],
                    c_send,
                    c_recv.at[h, p],
                    at_place(2 * t + odd),
                )

            span(DEV, send, 1)

    def relay(h, p):
        arrive(cbuf.at[h, p], c_recv.at[h, p])
        for t in range(TILES):
            lanes = slice(t * 128, (t + 1) * 128)
            for m in range(CPZ):
                scr[t, pl.ds(m, CPROWS, stride=CPZ), :] = cbuf[h, p, m, :, lanes].astype(f32)
            hbuf[h, p, :, :, lanes] = scr[t].reshape(ZN, PROWS, 128).astype(bf16)
        scatter_z(lambda t: hbuf.at[h, p, t], rx.at[h, p], h_send, h_recv.at[h, p])

    multiply(0, 0)
    multiply(0, 1)
    factor(2, 0)
    multiply(0, 2)
    give_back(0)
    below[...] = dot(order[...], gn[...], 0, 1).astype(bf16)
    factor(2, 1)
    relay(0, 0)
    multiply(1, 0)
    factor(2, 2)
    relay(0, 1)
    multiply(1, 1)
    relay(0, 2)
    multiply(1, 2)
    give_back(1)

    for p in range(NSTEP):
        relay(1, p)

    def grads_of(h, p, k1, k2):
        arrive(rx.at[h, p], h_recv.at[h, p])
        got = from_channels(rx.at[h, p])
        here = cells(p)
        return [(got * k1[here]).astype(bf16), (got * k2[here]).astype(bf16)]

    for p in range(NSTEP):
        here = cells(p)
        grads = jnp.concatenate(grads_of(0, p, a1, a2) + [gg[here]], axis=1)
        gz[here] = dot(grads, wcat[:, : 3 * CH], 1, 1)
        add_to(gwa, dot(zn[here], grads, 0, 0), p == 0)

    for t in range(DEV):
        k, at = divmod(t * EARLY, CH)
        source = gwo[at : at + EARLY, :] if k == 3 else gwa[at : at + EARLY, k * CH : (k + 1) * CH]
        epart[t] = source.astype(bf16)
    scatter("col", lambda t: epart.at[t], eg1, e_send.at[0], e_recv.at[0])

    def last(p):
        here = cells(p)
        grads = jnp.concatenate(grads_of(1, p, b1, b2), axis=1)
        total = gz[here] + dot(grads, wcat[:, 3 * CH :], 1, 1)
        add_to(gwb, dot(zn[here], grads, 0, 0), p == 0)
        add_to(lvec.at[0:1], column_sum(total * hat[here]), p == 0)
        add_to(lvec.at[1:2], column_sum(total), p == 0)
        return total

    def write(p, total):
        here = cells(p)
        value = norm_back(total * lg[...], hat[here], inv[here])
        gp[rows_of(p)] = value.astype(bf16).reshape(STEP, BLK, CH)

    write(0, last(0))
    write(1, last(1))
    total = last(2)

    vector = jnp.concatenate([lvec[...], jnp.zeros((8, CH), f32)], axis=0)
    for t in range(DEV):
        k, at = divmod(t * LATE, CH)
        source = gwb[at : at + LATE, k * CH : (k + 1) * CH]
        lpart[t] = jnp.concatenate([source, vector], axis=0).astype(bf16)
    scatter("col", lambda t: lpart.at[t], lg1, l_send.at[0], l_recv.at[0])
    arrive(eg1, e_recv.at[0])
    emid[...] = jnp.sum(eg1[...].astype(f32), axis=0).astype(bf16)
    scatter("row", lambda t: emid, eg2, e_send.at[1], e_recv.at[1])
    write(2, total)
    arrive(lg1, l_recv.at[0])
    lmid[...] = jnp.sum(lg1[...].astype(f32), axis=0).astype(bf16)
    scatter("row", lambda t: lmid, lg2, l_send.at[1], l_recv.at[1])
    arrive(eg2, e_recv.at[1])
    efin[...] = (jnp.sum(eg2[...].astype(f32), axis=0) * (1.0 / N)).astype(bf16)
    scatter("col", lambda t: efin, eout, e_send.at[2], e_recv.at[2])
    arrive(lg2, l_recv.at[1])
    done = jnp.sum(lg2[...].astype(f32), axis=0) * (1.0 / N)
    vout[...] = done[LATE:]
    lfin[...] = done[:LATE].astype(bf16)
    scatter("col", lambda t: lfin, lout, l_send.at[2], l_recv.at[2])

    for a in range(3):
        arrive(rbuf.at[a, :, 0 : ZN - 1], r_send.at[a])
    arrive(gq.at[:, 0, 0 : DEV - 1], g_send)
    for p in range(NSTEP):
        arrive(gq.at[p, 0], x_send.at[p])
    arrive(fq.at[:, :, 0 : DEV - 1], f_send)
    arrive(cbuf.at[:, :, 0 : DEV - 1], c_send)
    arrive(hbuf.at[:, :, 0 : ZN - 1], h_send)
    for k in range(3):
        arrive(eg1.at[0 : DEV - 1], e_send.at[k])
    arrive(lg1.at[0 : DEV - 1], l_send.at[0])
    arrive(lg2.at[0 : DEV - 1], l_send.at[1])
    arrive(lout.at[0 : DEV - 1], l_send.at[2])
    arrive(eout, e_recv.at[2])
    arrive(lout, l_recv.at[2])


def whole_step(*args):
    dma = pltpu.SemaphoreType.DMA
    turned = (NSTEP, ZN, PROWS, LANES)
    crossed = (2, NSTEP, DEV, CPROWS, LANES)
    flat = (BLK * BLK, CH)
    early = (DEV, EARLY, CH)
    late = (DEV, LATE + 16, CH)

    def wide(*shape):
        return pltpu.VMEM(shape, f32)

    def thin(*shape):
        return pltpu.VMEM(shape, bf16)

    return pl.pallas_call(
        kernel,
        in_specs=[pl.BlockSpec(memory_space=pl.ANY)] * 14,
        out_specs=[VMEM] * 4,
        out_shape=[
            jax.ShapeDtypeStruct((BLK, BLK, CH), bf16),
            jax.ShapeDtypeStruct(early, bf16),
            jax.ShapeDtypeStruct((DEV, LATE, CH), bf16),
            jax.ShapeDtypeStruct((16, CH), f32),
        ],
        scratch_shapes=[
            thin(*flat),
            wide(*flat),
            wide(*flat),
            wide(*flat),
            wide(*flat),
            wide(*flat),
            wide(*flat),
            thin(*flat),
            wide(*flat),
            wide(CH, CH),
            wide(CH, 3 * CH),
            wide(CH, 2 * CH),
            wide(8, CH),
            thin(CH, 5 * CH),
            thin(3, *turned),
            thin(2, *turned),
            thin(3, *turned),
            wide(TILES, ZN * PROWS, 128),
            thin(3, NSTEP, CPZ, CPROWS, LANES),
            thin(NSTEP, 2, DEV, CPROWS, LANES),
            thin(*crossed),
            wide(NT, PN, 128),
            thin(N, N),
            thin(N, N),
            thin(N, N),
            thin(N, N),
            thin(PN, N // 2),
            wide(NT // 2, N, 128),
            thin(*crossed),
            thin(*crossed),
            thin(2, *turned),
            thin(*early),
            thin(*early),
            thin(EARLY, CH),
            thin(*early),
            thin(EARLY, CH),
            thin(*late),
            thin(*late),
            thin(LATE + 16, CH),
            thin(*late),
            thin(LATE, CH),
            dma((3,)),
            dma((3, NSTEP)),
            dma,
            dma((NSTEP,)),
            dma((NSTEP,)),
            dma((NSTEP,)),
            dma,
            dma((2, NSTEP)),
            dma,
            dma((2, NSTEP)),
            dma,
            dma((2, NSTEP)),
            dma((3,)),
            dma((3,)),
            dma((3,)),
            dma((3,)),
            dma((14,)),
        ]
        + [pltpu.VMEM(a.shape, a.dtype) for a in args],
        name="whole_step",
        compiler_params=pltpu.CompilerParams(
            collective_id=1, has_side_effects=True, vmem_limit_bytes=LIMIT
        ),
    )(*args)


def finish_kernel(pair, early, late, vec, *outs):
    outs[0][...] = pair[...]
    place = (1, 2, 5, 6)
    for t in range(DEV):
        k, at = divmod(t * EARLY, CH)
        outs[place[k]][at : at + EARLY, :] = early[t].astype(f32)
        k, at = divmod(t * LATE, CH)
        outs[3 + k][at : at + LATE, :] = late[t].astype(f32)
    for k in range(4):
        outs[7 + k][...] = vec[k : k + 1]


def finish(*args):
    return pl.pallas_call(
        finish_kernel,
        in_specs=[VMEM] * 4,
        out_specs=[VMEM] * 11,
        out_shape=[jax.ShapeDtypeStruct((BLK, BLK, CH), bf16)]
        + [jax.ShapeDtypeStruct((CH, CH), f32)] * 6
        + [jax.ShapeDtypeStruct((1, CH), f32)] * 4,
        name="finish",
    )(*args)


def body(
    pair_map,
    saved_product,
    cotangent,
    residue_mask,
    ln_gain,
    ln_bias,
    out_gain,
    out_bias,
    *weights,
):
    vecs = [v.reshape(1, CH) for v in (ln_gain, ln_bias, out_gain, out_bias)]
    outs = finish(
        *whole_step(
            pair_map, saved_product, cotangent, residue_mask.reshape(NT, CH), *vecs, *weights
        )
    )
    return tuple(outs[:7]) + tuple(v.reshape(CH) for v in outs[7:])


def solution(mesh):
    return jax.shard_map(
        body,
        mesh=mesh,
        in_specs=(P("row", "col", None),) * 3 + (P(),) * 11,
        out_specs=(P("row", "col", None),) + (P(),) * 10,
        check_vma=False,
    )
```
